128 devices in a mesh: gx: 16 (over y, x), gy: 8 (over z, core).
Axes of the slice: x: 4, y: 4, z: 4, core: 2. Of those that a mesh axis runs over, the one named last changes fastest.
Arguments:
- right_side: float32 [256, 128, 512], P('gx', 'gy'), may hold values from -6 to 6
- point_counts: int32 [32, 16, 64], P('gx', 'gy'), may hold values from 0 to 64
Outputs:
- solution_field: float32 [256, 128, 512], P('gx', 'gy')
- residual: float32 [256, 128, 512], P('gx', 'gy')
The draws below stay inside these ranges and needn't reach their ends.
All inputs are finite; a program needn't handle non-finite values.
Results may differ from the reference program's by a relative error of at most 0.0003.
Values sent between devices are 32-bit elements; how exact they have to be, the bound alone decides.
No kernel may reach another device: no remote copies, remote signals or barrier semaphores. Data moves between devices by JAX's collectives and lax.ppermute only.
A program may use at most 512 MiB of HBM per device.

```python
import jax
import jax.numpy as jnp

BX = 2
BY = 2
BZ = 64
SWEEPS = 8
COARSE_SWEEPS = 8
NX = 256
NY = 128
NZ = 512
N_GX = 16
N_GY = 8


def set_ends(drawn, own_key, low, largest):
    place = [jax.random.randint(jax.random.fold_in(own_key, axis), (), 0, length) for axis, length in enumerate(drawn.shape)]
    main_axis = drawn.shape.index(max(drawn.shape))
    next_to = place[:main_axis] + [(place[main_axis] + 1) % drawn.shape[main_axis]] + place[main_axis + 1:]
    return drawn.at[tuple(place)].set(low).at[tuple(next_to)].set(largest)


def shard_levels(stream_key, shape, shards, low, high):
    gain, own = 1.0, jax.random.fold_in(stream_key, 6)
    for axis_at, shards_of in shards:
        draws = jnp.exp(jax.random.uniform(jax.random.fold_in(own, axis_at), (shards_of,), jnp.float32, low / len(shards), high / len(shards)))
        gain = gain * jnp.repeat(draws, shape[axis_at] // shards_of).reshape([-1 if axis == axis_at else 1 for axis in range(len(shape))])
    return gain


def bell_draw(own_key, extent, deviation, reach, split=(), kind=jnp.bfloat16):
    level = shard_levels(own_key, extent, split, -0.22, 0.18) if split else 1.0
    drawn = jax.random.normal(own_key, extent, jnp.float32) * deviation * level
    return jnp.minimum(jnp.maximum(drawn, -reach), reach).astype(kind)


def setup_inputs(seed: int = 0) -> dict:
    keys = jax.random.split(jax.random.key(seed), 3)
    return {
        "right_side": bell_draw(keys[0], (NX, NY, NZ), 1.0, 6.0, ((0, 16), (1, 8)), jnp.float32),
        "point_counts": set_ends(jax.random.randint(keys[1], (BX * N_GX, BY * N_GY, BZ), 0, 65), jax.random.fold_in(keys[1], 1), 0, 64).astype(jnp.int32),
    }


CENTER_W = 8.0 / 3.0
EDGE_W = 1.0 / 6.0
CORNER_W = 1.0 / 12.0
OMEGA = 2.0 / 3.0
SCREEN = 0.05


def expand(values, factor):
    first, second, third = values.shape
    grown = jnp.broadcast_to(values[:, None, :, None, :, None], (first, factor, second, factor, third, factor))
    return grown.reshape(first * factor, second * factor, third * factor)


def restrict(field):
    first, second, third = field.shape
    blocks = field.reshape(first // 2, 2, second // 2, 2, third // 2, 2)
    return 0.5 * jnp.sum(blocks, axis=(1, 3, 5))


def apply_padded(padded, field, screen):
    first, second, third = field.shape
    edges = jnp.zeros(field.shape, jnp.float32)
    corners = jnp.zeros(field.shape, jnp.float32)
    for shift_x in range(3):
        for shift_y in range(3):
            for shift_z in range(3):
                moved = abs(shift_x - 1) + abs(shift_y - 1) + abs(shift_z - 1)
                if moved < 2:
                    continue
                piece = padded[shift_x:shift_x + first, shift_y:shift_y + second, shift_z:shift_z + third]
                if moved == 2:
                    edges = edges + piece
                else:
                    corners = corners + piece
    return (CENTER_W + screen) * field - EDGE_W * edges - CORNER_W * corners


def relax(field, side, screen, sweeps):
    inverse = 1.0 / (CENTER_W + screen)
    for sweep in range(sweeps):
        image = apply_padded(jnp.pad(field, 1), field, screen)
        field = field + OMEGA * inverse * (side - image)
    return field


def reference(right_side, point_counts):
    brick_screen = point_counts.astype(jnp.float32) * SCREEN
    fine_screen = expand(brick_screen, 8)
    coarse_side = restrict(right_side)
    coarse_screen = expand(brick_screen * 4.0, 4)
    coarse = relax(jnp.zeros(coarse_side.shape, jnp.float32), coarse_side, coarse_screen, COARSE_SWEEPS)
    solution_field = relax(expand(coarse, 2), right_side, fine_screen, SWEEPS)
    image = apply_padded(jnp.pad(solution_field, 1), solution_field, fine_screen)
    return solution_field, right_side - image
```

```python
import jax
import jax.numpy as jnp
from jax import lax
from jax.experimental import pallas as pl
from jax.experimental.pallas import tpu as pltpu
from jax.sharding import PartitionSpec as P

CENTER = 8.0 / 3.0
OMEGA = 2.0 / 3.0
SCREEN = 0.05
THIRD = 1.0 - OMEGA
F32 = jnp.float32
HIGH = lax.Precision.HIGHEST
CHUNK = 4


def iota(shape, dim):
    return lax.broadcasted_iota(jnp.int32, shape, dim)


def pairing(rows, columns, factor, value):
    r, c = iota((rows, columns), 0), iota((rows, columns), 1)
    hit = (r // factor == c) if rows > columns else (c // factor == r)
    return jnp.where(hit, value, 0.0).astype(F32)


def stencil_rows(load, rows, blocks):
    v, t = {}, {}
    for x in range(rows[0] - 1, rows[-1] + 2):
        v[x] = load(x, 0)
        t[x] = [a + b for a, b in zip(load(x, -1), load(x, 1))]
    lane = iota(v[rows[0]][0].shape, 1)
    first, last = lane == 0, lane == 127
    zero = jnp.zeros(lane.shape, F32)
    out = {}
    for x in rows:
        m = [t[x - 1][b] + t[x + 1][b] for b in range(blocks)]
        w = [0.5 * m[b] + (t[x][b] + (v[x - 1][b] + v[x + 1][b])) for b in range(blocks)]
        up = [pltpu.roll(w[b], 1, 1) for b in range(blocks)]
        down = [pltpu.roll(w[b], 127, 1) for b in range(blocks)]
        total = []
        for b in range(blocks):
            below = jnp.where(first, up[b - 1] if b else zero, up[b])
            above = jnp.where(last, down[b + 1] if b < blocks - 1 else zero, down[b])
            total.append((below + above) + m[b])
        out[x] = total
    return v, out


def sweep(field, coupling, drive, source, base, chunks, tiles, blocks, brick, origin):
    def body(c, carry):
        x0 = base + c * CHUNK
        for tile in tiles:
            def load(x, shift):
                return [
                    field[source, x0 + x, b, pl.ds(8 * tile + shift, 8), :] for b in range(blocks)
                ]

            v, out = stencil_rows(load, range(CHUNK), blocks)
            for x in range(CHUNK):
                at = (x0 + x - origin) // brick
                for b in range(blocks):
                    new = (
                        THIRD * v[x][b]
                        + coupling[at, tile - 1, b] * out[x][b]
                        + drive[x0 + x, b, pl.ds(8 * tile, 8), :]
                    )
                    field[1 - source, x0 + x, b, pl.ds(8 * tile, 8), :] = new
        return carry

    lax.fori_loop(0, chunks, body, 0)


def restrict_kernel(side_ref, counts_ref, out_ref, tmp):
    for x in range(8):
        tmp[16 * x : 16 * x + 16, :] = side_ref[2 * x] + side_ref[2 * x + 1]
    halves = pairing(512, 256, 2, 0.5)
    rows = jnp.dot(pairing(64, 128, 2, 1.0), tmp[...], precision=HIGH, preferred_element_type=F32)
    coarse = jnp.dot(rows, halves, precision=HIGH, preferred_element_type=F32)
    for x in range(8):
        out_ref[x] = coarse[8 * x : 8 * x + 8, :]
    out_ref[8] = jnp.zeros((8, 256), F32)
    out_ref[8, 0:4, 0:64] = counts_ref[...].reshape(4, 64).astype(F32)


def in_domain(index, low, count):
    place = low + index - 1
    return jnp.where((place >= 0) & (place < count), 1.0, 0.0).astype(F32)


def coarse_kernel(mid_ref, low_ref, high_ref, c_ref, top_ref, bottom_ref, inv_ref, center_ref,
                  field, drive, coupling):
    gx, gy = lax.axis_index("gx"), lax.axis_index("gy")
    n_gx, n_gy = lax.axis_size("gx"), lax.axis_size("gy")
    strips = (low_ref, mid_ref, high_ref)
    counts = jnp.concatenate([strips[j][9 * i + 8][:, 0:64] for i in range(3) for j in range(3)], axis=0)
    spread = jnp.dot(counts, pairing(64, 256, 4, 1.0), precision=HIGH, preferred_element_type=F32)
    weight = OMEGA / (CENTER + (SCREEN * 4.0) * spread)
    sub = iota((8, 128), 0)
    zero = jnp.zeros((8, 128), F32)
    for x in range(26):
        for b in range(2):
            for parity in range(2):
                field[parity, x, b, 0:8, :] = zero
                field[parity, x, b, 32:40, :] = zero
                if x in (0, 25):
                    for tile in (1, 2, 3):
                        field[parity, x, b, 8 * tile : 8 * tile + 8, :] = zero
    for i in range(3):
        for j in range(3):
            inside = in_domain(i, gx, n_gx) * in_domain(j, gy, n_gy)
            group = weight[8 * (3 * i + j) : 8 * (3 * i + j) + 8, :] * inside
            for k in range(2):
                for b in range(2):
                    lanes = slice(128 * b, 128 * b + 128)
                    tile = jnp.where(
                        sub < 4,
                        jnp.broadcast_to(group[2 * k : 2 * k + 1, lanes], (8, 128)),
                        jnp.broadcast_to(group[2 * k + 1 : 2 * k + 2, lanes], (8, 128)),
                    )
                    coupling[2 * i + k, j, b] = tile * (1.0 / 6.0)
                    for x in range(4):
                        at = 8 * i + 4 * k + x
                        value = tile * strips[j][9 * i + 4 * k + x, :, lanes]
                        drive[at + 1, b, pl.ds(8 * j + 8, 8), :] = value
                        field[0, at + 1, b, pl.ds(8 * j + 8, 8), :] = value

    def step(k, carry):
        half = k // 2
        sweep(field, coupling, drive, k % 2, 3 + 2 * half, 5 - half, (1, 2, 3), 2, 4, 1)
        return carry

    lax.fori_loop(0, 7, step, 0)
    for x in range(8):
        row = jnp.concatenate([field[1, 9 + x, b, 16:24, :] for b in range(2)], axis=1)
        c_ref[x] = row
        if x < 5:
            bottom_ref[x] = row
        if x >= 3:
            top_ref[x - 3] = row

    wide = jnp.dot(counts, pairing(64, 512, 8, 1.0), precision=HIGH, preferred_element_type=F32)
    center = CENTER + SCREEN * wide
    inverse = OMEGA / center
    for xb in range(4):
        i, k = ((xb + 1) // 2, (xb + 1) % 2)
        for yb in range(4):
            j, l = ((yb + 1) // 2, (yb + 1) % 2)
            at = 8 * (3 * i + j) + 2 * k + l
            inside = in_domain(i, gx, n_gx) * in_domain(j, gy, n_gy)
            inv_ref[xb, yb : yb + 1, :] = inverse[at : at + 1, :] * inside
            center_ref[xb, yb : yb + 1, :] = center[at : at + 1, :]


def fine_kernel(side_ref, side_low, side_high, c_ref, c_low, c_high, inv_ref, center_ref, solution_ref, residual_ref,
                field, drive, coupling):
    gx, gy = lax.axis_index("gx"), lax.axis_index("gy")
    n_gx, n_gy = lax.axis_size("gx"), lax.axis_size("gy")
    zero = jnp.zeros((8, 128), F32)
    for x in range(36):
        for b in range(4):
            field[1, x, b, 0:8, :] = zero
            field[1, x, b, 40:48, :] = zero
            if x in (0, 1, 34, 35):
                for tile in (1, 2, 3, 4):
                    field[1, x, b, 8 * tile : 8 * tile + 8, :] = zero
    doubling = pairing(256, 512, 2, 1.0)
    for j, ref in enumerate((c_low, c_ref, c_high)):
        here = in_domain(j, gy, n_gy)
        rows = []
        for x in range(18):
            i = 0 if x < 5 else (1 if x < 13 else 2)
            rows.append(ref[x] * (here * in_domain(i, gx, n_gx)))
        grown = jnp.dot(jnp.concatenate(rows, axis=0), doubling, precision=HIGH, preferred_element_type=F32)
        for x in range(18):
            for b in range(4):
                value = grown[8 * x : 8 * x + 8, 128 * b : 128 * b + 128]
                for dx in range(2):
                    for dy in range(2):
                        field[0, 2 * x + dx, b, pl.ds(16 * j + dy, 8, stride=2), :] = value
    for xb in range(4):
        for yb in range(4):
            for b in range(4):
                tile = jnp.broadcast_to(inv_ref[xb, yb : yb + 1, 128 * b : 128 * b + 128], (8, 128))
                coupling[xb, yb, b] = tile * (1.0 / 6.0)
                source = (side_low, side_ref, side_ref, side_high)[yb]
                row = (0, 0, 8, 0)[yb]

                def fill(x, carry, tile=tile, source=source, row=row, b=b, xb=xb, yb=yb):
                    at = 8 * xb + x
                    drive[at + 2, b, pl.ds(8 * yb + 8, 8), :] = (
                        tile * source[at, row : row + 8, 128 * b : 128 * b + 128]
                    )
                    return carry

                lax.fori_loop(0, 8, fill, 0, unroll=True)

    def step(k, carry):
        half = k // 2
        sweep(field, coupling, drive, k % 2, 2 + 2 * half, 8 - half, (1, 2, 3, 4), 4, 8, 2)
        return carry

    lax.fori_loop(0, 8, step, 0)

    def finish(c, carry):
        x0 = c * CHUNK
        for tile in (2, 3):
            def load(x, shift):
                return [field[0, x0 + 10 + x, b, pl.ds(8 * tile + shift, 8), :] for b in range(4)]

            v, out = stencil_rows(load, range(CHUNK), 4)
            for x in range(CHUNK):
                brick = 1 + (x0 + x) // 8
                for b in range(4):
                    lanes = slice(128 * b, 128 * b + 128)
                    rows = slice(8 * tile - 16, 8 * tile - 8)
                    center = center_ref[brick, tile - 1 : tile, lanes]
                    solution_ref[x0 + x, rows, lanes] = v[x][b]
                    residual_ref[x0 + x, rows, lanes] = (
                        side_ref[x0 + x + 8, rows, lanes] - center * v[x][b] + (1.0 / 6.0) * out[x][b]
                    )
        return carry

    lax.fori_loop(0, 16 // CHUNK, finish, 0)


def shape(*dims):
    return jax.ShapeDtypeStruct(dims, F32)


def shards(right_side, point_counts):
    params = pltpu.CompilerParams(vmem_limit_bytes=24 * 1024 * 1024)
    n_gx, n_gy = lax.axis_size("gx"), lax.axis_size("gy")

    def move(value, axis, step):
        count = n_gx if axis == "gx" else n_gy
        return lax.ppermute(value, axis, [(i, (i + step) % count) for i in range(count)])

    packed = pl.pallas_call(
        restrict_kernel,
        out_shape=shape(9, 8, 256),
        scratch_shapes=[pltpu.VMEM((128, 512), F32)],
        compiler_params=params,
        name="restrict",
    )(right_side, point_counts)
    packed = jnp.concatenate([move(packed, "gx", 1), packed, move(packed, "gx", -1)], axis=0)
    coarse, top, bottom, inverse, center = pl.pallas_call(
        coarse_kernel,
        out_shape=[shape(8, 8, 256), shape(5, 8, 256), shape(5, 8, 256), shape(4, 4, 512), shape(4, 4, 512)],
        scratch_shapes=[
            pltpu.VMEM((2, 26, 2, 40, 128), F32),
            pltpu.VMEM((26, 2, 40, 128), F32),
            pltpu.VMEM((6, 3, 2, 8, 128), F32),
        ],
        compiler_params=params,
        name="coarse",
    )(packed, move(packed, "gy", 1), move(packed, "gy", -1))
    coarse = jnp.concatenate([move(top, "gx", 1), coarse, move(bottom, "gx", -1)], axis=0)
    side = jnp.concatenate(
        [move(right_side[8:16], "gx", 1), right_side, move(right_side[0:8], "gx", -1)], axis=0
    )
    solution_field, residual = pl.pallas_call(
        fine_kernel,
        out_shape=[shape(16, 16, 512), shape(16, 16, 512)],
        scratch_shapes=[
            pltpu.VMEM((2, 36, 4, 48, 128), F32),
            pltpu.VMEM((36, 4, 48, 128), F32),
            pltpu.VMEM((4, 4, 4, 8, 128), F32),
        ],
        compiler_params=params,
        name="fine",
    )(
        side,
        move(side[:, 8:16], "gy", 1),
        move(side[:, 0:8], "gy", -1),
        coarse,
        move(coarse, "gy", 1),
        move(coarse, "gy", -1),
        inverse,
        center,
    )
    return solution_field, residual


def solution(mesh):
    specs = (P("gx", "gy", None), P("gx", "gy", None))
    return jax.shard_map(shards, mesh=mesh, in_specs=specs, out_specs=specs, check_vma=False)
```

```python
import jax
import jax.numpy as jnp
from jax import lax
from jax.experimental import pallas as pl
from jax.experimental.pallas import tpu as pltpu
from jax.sharding import PartitionSpec as P

CENTER = 8.0 / 3.0
OMEGA = 2.0 / 3.0
SCREEN = 0.05
THIRD = 1.0 - OMEGA
F32 = jnp.float32
HIGH = lax.Precision.HIGHEST
CHUNK = 4


def iota(shape, dim):
    return lax.broadcasted_iota(jnp.int32, shape, dim)


def pairing(rows, columns, factor, value):
    r, c = iota((rows, columns), 0), iota((rows, columns), 1)
    hit = (r // factor == c) if rows > columns else (c // factor == r)
    return jnp.where(hit, value, 0.0).astype(F32)


def stencil_rows(load, rows, blocks):
    v, t = {}, {}
    for x in range(rows[0] - 1, rows[-1] + 2):
        v[x] = load(x, 0)
        t[x] = [a + b for a, b in zip(load(x, -1), load(x, 1))]
    lane = iota(v[rows[0]][0].shape, 1)
    first, last = lane == 0, lane == 127
    zero = jnp.zeros(lane.shape, F32)
    out = {}
    for x in rows:
        m = [t[x - 1][b] + t[x + 1][b] for b in range(blocks)]
        w = [0.5 * m[b] + (t[x][b] + (v[x - 1][b] + v[x + 1][b])) for b in range(blocks)]
        up = [pltpu.roll(w[b], 1, 1) for b in range(blocks)]
        down = [pltpu.roll(w[b], 127, 1) for b in range(blocks)]
        total = []
        for b in range(blocks):
            below = jnp.where(first, up[b - 1] if b else zero, up[b])
            above = jnp.where(last, down[b + 1] if b < blocks - 1 else zero, down[b])
            total.append((below + above) + m[b])
        out[x] = total
    return v, out


def sweep(source, target, coupling, drive, base, chunks, tiles, blocks, log_brick, origin):
    def body(c, carry):
        x0 = base + c * CHUNK
        for tile in tiles:
            def load(x, shift):
                return [
                    source[x0 + x, b, pl.ds(8 * tile + shift, 8), :] for b in range(blocks)
                ]

            v, out = stencil_rows(load, range(CHUNK), blocks)
            for x in range(CHUNK):
                at = lax.shift_right_logical(x0 + x - origin, log_brick)
                for b in range(blocks):
                    new = (
                        THIRD * v[x][b]
                        + coupling[at, tile - 1, b] * out[x][b]
                        + drive[x0 + x, b, pl.ds(8 * tile, 8), :]
                    )
                    target[x0 + x, b, pl.ds(8 * tile, 8), :] = new
        return carry

    lax.fori_loop(0, chunks, body, 0)


def restrict_kernel(side_ref, counts_ref, out_ref, tmp):
    for x in range(8):
        tmp[16 * x : 16 * x + 16, :] = side_ref[2 * x] + side_ref[2 * x + 1]
    halves = pairing(512, 256, 2, 0.5)
    rows = jnp.dot(pairing(64, 128, 2, 1.0), tmp[...], precision=HIGH, preferred_element_type=F32)
    coarse = jnp.dot(rows, halves, precision=HIGH, preferred_element_type=F32)
    for x in range(8):
        out_ref[x] = coarse[8 * x : 8 * x + 8, :]
    out_ref[8] = jnp.zeros((8, 256), F32)
    out_ref[8, 0:4, 0:64] = counts_ref[...].reshape(4, 64).astype(F32)


def in_domain(index, low, count):
    place = low + index - 1
    return jnp.where((place >= 0) & (place < count), 1.0, 0.0).astype(F32)


def coarse_kernel(mid_ref, low_ref, high_ref, c_ref, top_ref, bottom_ref, inv_ref, center_ref,
                  even, odd, drive, coupling):
    gx, gy = lax.axis_index("gx"), lax.axis_index("gy")
    n_gx, n_gy = lax.axis_size("gx"), lax.axis_size("gy")
    strips = (low_ref, mid_ref, high_ref)
    counts = jnp.concatenate([strips[j][9 * i + 8][:, 0:64] for i in range(3) for j in range(3)], axis=0)
    spread = jnp.dot(counts, pairing(64, 256, 4, 1.0), precision=HIGH, preferred_element_type=F32)
    weight = OMEGA / (CENTER + (SCREEN * 4.0) * spread)
    sub = iota((8, 128), 0)
    zero = jnp.zeros((8, 128), F32)
    for x in range(26):
        for b in range(2):
            for field in (even, odd):
                field[x, b, 0:8, :] = zero
                field[x, b, 32:40, :] = zero
                if x in (0, 25):
                    for tile in (1, 2, 3):
                        field[x, b, 8 * tile : 8 * tile + 8, :] = zero
    for i in range(3):
        for j in range(3):
            inside = in_domain(i, gx, n_gx) * in_domain(j, gy, n_gy)
            group = weight[8 * (3 * i + j) : 8 * (3 * i + j) + 8, :] * inside
            for k in range(2):
                for b in range(2):
                    lanes = slice(128 * b, 128 * b + 128)
                    tile = jnp.where(
                        sub < 4,
                        jnp.broadcast_to(group[2 * k : 2 * k + 1, lanes], (8, 128)),
                        jnp.broadcast_to(group[2 * k + 1 : 2 * k + 2, lanes], (8, 128)),
                    )
                    coupling[2 * i + k, j, b] = tile * (1.0 / 6.0)
                    for x in range(4):
                        at = 8 * i + 4 * k + x
                        value = tile * strips[j][9 * i + 4 * k + x, :, lanes]
                        drive[at + 1, b, pl.ds(8 * j + 8, 8), :] = value
                        even[at + 1, b, pl.ds(8 * j + 8, 8), :] = value

    def step(k, carry):
        sweep(even, odd, coupling, drive, 3 + 2 * k, 5 - k, (1, 2, 3), 2, 2, 1)
        sweep(odd, even, coupling, drive, 3 + 2 * k, 5 - k, (1, 2, 3), 2, 2, 1)
        return carry

    lax.fori_loop(0, 3, step, 0)
    sweep(even, odd, coupling, drive, 9, 2, (2,), 2, 2, 1)
    for x in range(8):
        row = jnp.concatenate([odd[9 + x, b, 16:24, :] for b in range(2)], axis=1)
        c_ref[x] = row
        if x < 5:
            bottom_ref[x] = row
        if x >= 3:
            top_ref[x - 3] = row

    wide = jnp.dot(counts, pairing(64, 512, 8, 1.0), precision=HIGH, preferred_element_type=F32)
    center = CENTER + SCREEN * wide
    inverse = OMEGA / center
    for xb in range(4):
        i, k = ((xb + 1) // 2, (xb + 1) % 2)
        for yb in range(4):
            j, l = ((yb + 1) // 2, (yb + 1) % 2)
            at = 8 * (3 * i + j) + 2 * k + l
            inside = in_domain(i, gx, n_gx) * in_domain(j, gy, n_gy)
            inv_ref[xb, yb : yb + 1, :] = inverse[at : at + 1, :] * inside
            center_ref[xb, yb : yb + 1, :] = center[at : at + 1, :]


def fine_kernel(side_ref, side_low, side_high, c_ref, c_low, c_high, inv_ref, center_ref, solution_ref, residual_ref,
                even, odd, drive, coupling):
    gx, gy = lax.axis_index("gx"), lax.axis_index("gy")
    n_gx, n_gy = lax.axis_size("gx"), lax.axis_size("gy")
    zero = jnp.zeros((8, 128), F32)
    for x in range(36):
        for b in range(4):
            odd[x, b, 0:8, :] = zero
            odd[x, b, 40:48, :] = zero
            if x in (0, 1, 34, 35):
                for tile in (1, 2, 3, 4):
                    odd[x, b, 8 * tile : 8 * tile + 8, :] = zero
    doubling = pairing(256, 512, 2, 1.0)
    for j, ref in enumerate((c_low, c_ref, c_high)):
        here = in_domain(j, gy, n_gy)
        rows = []
        for x in range(18):
            i = 0 if x < 5 else (1 if x < 13 else 2)
            rows.append(ref[x] * (here * in_domain(i, gx, n_gx)))
        grown = jnp.dot(jnp.concatenate(rows, axis=0), doubling, precision=HIGH, preferred_element_type=F32)
        for x in range(18):
            for b in range(4):
                value = grown[8 * x : 8 * x + 8, 128 * b : 128 * b + 128]
                for dx in range(2):
                    for dy in range(2):
                        even[2 * x + dx, b, pl.ds(16 * j + dy, 8, stride=2), :] = value
    for xb in range(4):
        for yb in range(4):
            for b in range(4):
                tile = jnp.broadcast_to(inv_ref[xb, yb : yb + 1, 128 * b : 128 * b + 128], (8, 128))
                coupling[xb, yb, b] = tile * (1.0 / 6.0)
                source = (side_low, side_ref, side_ref, side_high)[yb]
                row = (0, 0, 8, 0)[yb]

                def fill(x, carry, tile=tile, source=source, row=row, b=b, xb=xb, yb=yb):
                    at = 8 * xb + x
                    drive[at + 2, b, pl.ds(8 * yb + 8, 8), :] = (
                        tile * source[at, row : row + 8, 128 * b : 128 * b + 128]
                    )
                    return carry

                lax.fori_loop(0, 8, fill, 0, unroll=True)

    def step(k, carry):
        sweep(even, odd, coupling, drive, 2 + 2 * k, 8 - k, (1, 2, 3, 4), 4, 3, 2)
        sweep(odd, even, coupling, drive, 2 + 2 * k, 8 - k, (1, 2, 3, 4), 4, 3, 2)
        return carry

    lax.fori_loop(0, 4, step, 0)

    def finish(c, carry):
        x0 = c * CHUNK
        for tile in (2, 3):
            def load(x, shift):
                return [even[x0 + 10 + x, b, pl.ds(8 * tile + shift, 8), :] for b in range(4)]

            v, out = stencil_rows(load, range(CHUNK), 4)
            for x in range(CHUNK):
                brick = 1 + lax.shift_right_logical(x0 + x, 3)
                for b in range(4):
                    lanes = slice(128 * b, 128 * b + 128)
                    rows = slice(8 * tile - 16, 8 * tile - 8)
                    center = center_ref[brick, tile - 1 : tile, lanes]
                    solution_ref[x0 + x, rows, lanes] = v[x][b]
                    residual_ref[x0 + x, rows, lanes] = (
                        side_ref[x0 + x + 8, rows, lanes] - center * v[x][b] + (1.0 / 6.0) * out[x][b]
                    )
        return carry

    lax.fori_loop(0, 16 // CHUNK, finish, 0)


def shape(*dims):
    return jax.ShapeDtypeStruct(dims, F32)


def shards(right_side, point_counts):
    params = pltpu.CompilerParams(vmem_limit_bytes=24 * 1024 * 1024)
    n_gx, n_gy = lax.axis_size("gx"), lax.axis_size("gy")

    def move(value, axis, step):
        count = n_gx if axis == "gx" else n_gy
        return lax.ppermute(value, axis, [(i, (i + step) % count) for i in range(count)])

    packed = pl.pallas_call(
        restrict_kernel,
        out_shape=shape(9, 8, 256),
        scratch_shapes=[pltpu.VMEM((128, 512), F32)],
        compiler_params=params,
        name="restrict",
    )(right_side, point_counts)
    packed = jnp.concatenate([move(packed, "gx", 1), packed, move(packed, "gx", -1)], axis=0)
    coarse, top, bottom, inverse, center = pl.pallas_call(
        coarse_kernel,
        out_shape=[shape(8, 8, 256), shape(5, 8, 256), shape(5, 8, 256), shape(4, 4, 512), shape(4, 4, 512)],
        scratch_shapes=[
            pltpu.VMEM((26, 2, 40, 128), F32),
            pltpu.VMEM((26, 2, 40, 128), F32),
            pltpu.VMEM((26, 2, 40, 128), F32),
            pltpu.VMEM((6, 3, 2, 8, 128), F32),
        ],
        compiler_params=params,
        name="coarse",
    )(packed, move(packed, "gy", 1), move(packed, "gy", -1))
    coarse = jnp.concatenate([move(top, "gx", 1), coarse, move(bottom, "gx", -1)], axis=0)
    side = jnp.concatenate(
        [move(right_side[8:16], "gx", 1), right_side, move(right_side[0:8], "gx", -1)], axis=0
    )
    solution_field, residual = pl.pallas_call(
        fine_kernel,
        out_shape=[shape(16, 16, 512), shape(16, 16, 512)],
        scratch_shapes=[
            pltpu.VMEM((36, 4, 48, 128), F32),
            pltpu.VMEM((36, 4, 48, 128), F32),
            pltpu.VMEM((36, 4, 48, 128), F32),
            pltpu.VMEM((4, 4, 4, 8, 128), F32),
        ],
        compiler_params=params,
        name="fine",
    )(
        side,
        move(side[:, 8:16], "gy", 1),
        move(side[:, 0:8], "gy", -1),
        coarse,
        move(coarse, "gy", 1),
        move(coarse, "gy", -1),
        inverse,
        center,
    )
    return solution_field, residual


def solution(mesh):
    specs = (P("gx", "gy", None), P("gx", "gy", None))
    return jax.shard_map(shards, mesh=mesh, in_specs=specs, out_specs=specs, check_vma=False)
```

```python
import jax
import jax.numpy as jnp
from jax import lax
from jax.experimental import pallas as pl
from jax.experimental.pallas import tpu as pltpu
from jax.sharding import PartitionSpec as P

CENTER = 8.0 / 3.0
OMEGA = 2.0 / 3.0
SCREEN = 0.05
THIRD = 1.0 - OMEGA
F32 = jnp.float32
HIGH = lax.Precision.HIGHEST
CHUNK = 8
FINE_PARTS = 1
COARSE_PARTS = 1


def iota(shape, dim):
    return lax.broadcasted_iota(jnp.int32, shape, dim)


def pairing(rows, columns, factor, value):
    r, c = iota((rows, columns), 0), iota((rows, columns), 1)
    hit = (r // factor == c) if rows > columns else (c // factor == r)
    return jnp.where(hit, value, 0.0).astype(F32)


def stencil_rows(load, rows, blocks):
    v, t = {}, {}
    for x in range(rows[0] - 1, rows[-1] + 2):
        v[x] = load(x, 0)
        t[x] = [a + b for a, b in zip(load(x, -1), load(x, 1))]
    lane = iota(v[rows[0]][0].shape, 1)
    first, last = lane == 0, lane == 127
    zero = jnp.zeros(lane.shape, F32)
    out = {}
    for x in rows:
        m = [t[x - 1][b] + t[x + 1][b] for b in range(blocks)]
        w = [0.5 * m[b] + (t[x][b] + (v[x - 1][b] + v[x + 1][b])) for b in range(blocks)]
        up = [pltpu.roll(w[b], 1, 1) for b in range(blocks)]
        down = [pltpu.roll(w[b], 127, 1) for b in range(blocks)]
        total = []
        for b in range(blocks):
            below = jnp.where(first, up[b - 1] if b else zero, up[b])
            above = jnp.where(last, down[b + 1] if b < blocks - 1 else zero, down[b])
            total.append((below + above) + m[b])
        out[x] = total
    return v, out


def sweep(source, target, coupling, drive, base, rows, parts, tiles, blocks, log_brick, origin):
    step = rows // parts

    def body(c, carry):
        x0 = base + c * step
        for tile in tiles:
            def load(x, shift):
                return [source[x0 + x, b, pl.ds(8 * tile + shift, 8), :] for b in range(blocks)]

            v, out = stencil_rows(load, range(step), blocks)
            for x in range(step):
                at = x0 + x - origin
                at = at >> log_brick if parts == 1 else lax.shift_right_logical(at, log_brick)
                for b in range(blocks):
                    target[x0 + x, b, pl.ds(8 * tile, 8), :] = (
                        THIRD * v[x][b]
                        + coupling[at, tile - 1, b] * out[x][b]
                        + drive[x0 + x, b, pl.ds(8 * tile, 8), :]
                    )
        return carry

    if parts == 1:
        body(0, 0)
    else:
        lax.fori_loop(0, parts, body, 0)


def restrict_kernel(side_ref, counts_ref, out_ref, tmp):
    for x in range(8):
        tmp[16 * x : 16 * x + 16, :] = side_ref[2 * x] + side_ref[2 * x + 1]
    halves = pairing(512, 256, 2, 0.5)
    rows = jnp.dot(pairing(64, 128, 2, 1.0), tmp[...], precision=HIGH, preferred_element_type=F32)
    coarse = jnp.dot(rows, halves, precision=HIGH, preferred_element_type=F32)
    for x in range(8):
        out_ref[x] = coarse[8 * x : 8 * x + 8, :]
    out_ref[8] = jnp.zeros((8, 256), F32)
    out_ref[8, 0:4, 0:64] = counts_ref[...].reshape(4, 64).astype(F32)


def in_domain(index, low, count):
    place = low + index - 1
    return jnp.where((place >= 0) & (place < count), 1.0, 0.0).astype(F32)


def coarse_kernel(mid_ref, low_ref, high_ref, c_ref, top_ref, bottom_ref, inv_ref, center_ref,
                  even, odd, drive, coupling):
    gx, gy = lax.axis_index("gx"), lax.axis_index("gy")
    n_gx, n_gy = lax.axis_size("gx"), lax.axis_size("gy")
    strips = (low_ref, mid_ref, high_ref)
    counts = jnp.concatenate([strips[j][9 * i + 8][:, 0:64] for i in range(3) for j in range(3)], axis=0)
    spread = jnp.dot(counts, pairing(64, 256, 4, 1.0), precision=HIGH, preferred_element_type=F32)
    weight = OMEGA / (CENTER + (SCREEN * 4.0) * spread)
    sub = iota((8, 128), 0)
    zero = jnp.zeros((8, 128), F32)
    for x in range(26):
        for b in range(2):
            for field in (even, odd):
                field[x, b, 0:8, :] = zero
                field[x, b, 32:40, :] = zero
                if x in (0, 25):
                    for tile in (1, 2, 3):
                        field[x, b, 8 * tile : 8 * tile + 8, :] = zero
    for i in range(3):
        for j in range(3):
            inside = in_domain(i, gx, n_gx) * in_domain(j, gy, n_gy)
            group = weight[8 * (3 * i + j) : 8 * (3 * i + j) + 8, :] * inside
            for k in range(2):
                for b in range(2):
                    lanes = slice(128 * b, 128 * b + 128)
                    tile = jnp.where(
                        sub < 4,
                        jnp.broadcast_to(group[2 * k : 2 * k + 1, lanes], (8, 128)),
                        jnp.broadcast_to(group[2 * k + 1 : 2 * k + 2, lanes], (8, 128)),
                    )
                    coupling[2 * i + k, j, b] = tile * (1.0 / 6.0)
                    for x in range(4):
                        at = 8 * i + 4 * k + x
                        value = tile * strips[j][9 * i + 4 * k + x, :, lanes]
                        drive[at + 1, b, pl.ds(8 * j + 8, 8), :] = value
                        even[at + 1, b, pl.ds(8 * j + 8, 8), :] = value

    for k in range(7):
        source, target = (even, odd) if k % 2 == 0 else (odd, even)
        halo = 6 - k
        tiles = (1, 2, 3) if halo else (2,)
        sweep(source, target, coupling, drive, 9 - halo, 8 + 2 * halo, COARSE_PARTS, tiles, 2, 2, 1)
    for x in range(8):
        row = jnp.concatenate([odd[9 + x, b, 16:24, :] for b in range(2)], axis=1)
        c_ref[x] = row
        if x < 5:
            bottom_ref[x] = row
        if x >= 3:
            top_ref[x - 3] = row

    wide = jnp.dot(counts, pairing(64, 512, 8, 1.0), precision=HIGH, preferred_element_type=F32)
    center = CENTER + SCREEN * wide
    inverse = OMEGA / center
    for xb in range(4):
        i, k = ((xb + 1) // 2, (xb + 1) % 2)
        for yb in range(4):
            j, l = ((yb + 1) // 2, (yb + 1) % 2)
            at = 8 * (3 * i + j) + 2 * k + l
            inside = in_domain(i, gx, n_gx) * in_domain(j, gy, n_gy)
            inv_ref[xb, yb : yb + 1, :] = inverse[at : at + 1, :] * inside
            center_ref[xb, yb : yb + 1, :] = center[at : at + 1, :]


def fine_kernel(side_ref, side_low, side_high, c_ref, c_low, c_high, inv_ref, center_ref, solution_ref, residual_ref,
                even, odd, drive, coupling):
    gx, gy = lax.axis_index("gx"), lax.axis_index("gy")
    n_gx, n_gy = lax.axis_size("gx"), lax.axis_size("gy")
    zero = jnp.zeros((8, 128), F32)
    for x in range(36):
        for b in range(4):
            odd[x, b, 0:8, :] = zero
            odd[x, b, 40:48, :] = zero
            if x in (0, 1, 34, 35):
                for tile in (1, 2, 3, 4):
                    odd[x, b, 8 * tile : 8 * tile + 8, :] = zero
    doubling = pairing(256, 512, 2, 1.0)
    for j, ref in enumerate((c_low, c_ref, c_high)):
        here = in_domain(j, gy, n_gy)
        rows = []
        for x in range(18):
            i = 0 if x < 5 else (1 if x < 13 else 2)
            rows.append(ref[x] * (here * in_domain(i, gx, n_gx)))
        grown = jnp.dot(jnp.concatenate(rows, axis=0), doubling, precision=HIGH, preferred_element_type=F32)
        for x in range(18):
            for b in range(4):
                value = grown[8 * x : 8 * x + 8, 128 * b : 128 * b + 128]
                for dx in range(2):
                    for dy in range(2):
                        even[2 * x + dx, b, pl.ds(16 * j + dy, 8, stride=2), :] = value
    for xb in range(4):
        for yb in range(4):
            for b in range(4):
                tile = jnp.broadcast_to(inv_ref[xb, yb : yb + 1, 128 * b : 128 * b + 128], (8, 128))
                coupling[xb, yb, b] = tile * (1.0 / 6.0)
                source = (side_low, side_ref, side_ref, side_high)[yb]
                row = (0, 0, 8, 0)[yb]

                def fill(x, carry, tile=tile, source=source, row=row, b=b, xb=xb, yb=yb):
                    at = 8 * xb + x
                    drive[at + 2, b, pl.ds(8 * yb + 8, 8), :] = (
                        tile * source[at, row : row + 8, 128 * b : 128 * b + 128]
                    )
                    return carry

                lax.fori_loop(0, 8, fill, 0, unroll=True)

    for k in range(8):
        source, target = (even, odd) if k % 2 == 0 else (odd, even)
        halo = 8 - k
        sweep(source, target, coupling, drive, 10 - halo, 16 + 2 * halo, FINE_PARTS, (1, 2, 3, 4), 4, 3, 2)

    def finish(c, carry):
        x0 = c * CHUNK
        for tile in (2, 3):
            def load(x, shift):
                return [even[x0 + 10 + x, b, pl.ds(8 * tile + shift, 8), :] for b in range(4)]

            v, out = stencil_rows(load, range(CHUNK), 4)
            for x in range(CHUNK):
                brick = 1 + lax.shift_right_logical(x0 + x, 3)
                for b in range(4):
                    lanes = slice(128 * b, 128 * b + 128)
                    rows = slice(8 * tile - 16, 8 * tile - 8)
                    center = center_ref[brick, tile - 1 : tile, lanes]
                    solution_ref[x0 + x, rows, lanes] = v[x][b]
                    residual_ref[x0 + x, rows, lanes] = (
                        side_ref[x0 + x + 8, rows, lanes] - center * v[x][b] + (1.0 / 6.0) * out[x][b]
                    )
        return carry

    lax.fori_loop(0, 16 // CHUNK, finish, 0)


def shape(*dims):
    return jax.ShapeDtypeStruct(dims, F32)


def shards(right_side, point_counts):
    params = pltpu.CompilerParams(vmem_limit_bytes=24 * 1024 * 1024)
    n_gx, n_gy = lax.axis_size("gx"), lax.axis_size("gy")

    def move(value, axis, step):
        count = n_gx if axis == "gx" else n_gy
        return lax.ppermute(value, axis, [(i, (i + step) % count) for i in range(count)])

    packed = pl.pallas_call(
        restrict_kernel,
        out_shape=shape(9, 8, 256),
        scratch_shapes=[pltpu.VMEM((128, 512), F32)],
        compiler_params=params,
        name="restrict",
    )(right_side, point_counts)
    packed = jnp.concatenate([move(packed, "gx", 1), packed, move(packed, "gx", -1)], axis=0)
    coarse, top, bottom, inverse, center = pl.pallas_call(
        coarse_kernel,
        out_shape=[shape(8, 8, 256), shape(5, 8, 256), shape(5, 8, 256), shape(4, 4, 512), shape(4, 4, 512)],
        scratch_shapes=[
            pltpu.VMEM((26, 2, 40, 128), F32),
            pltpu.VMEM((26, 2, 40, 128), F32),
            pltpu.VMEM((26, 2, 40, 128), F32),
            pltpu.VMEM((6, 3, 2, 8, 128), F32),
        ],
        compiler_params=params,
        name="coarse",
    )(packed, move(packed, "gy", 1), move(packed, "gy", -1))
    coarse = jnp.concatenate([move(top, "gx", 1), coarse, move(bottom, "gx", -1)], axis=0)
    side = jnp.concatenate(
        [move(right_side[8:16], "gx", 1), right_side, move(right_side[0:8], "gx", -1)], axis=0
    )
    solution_field, residual = pl.pallas_call(
        fine_kernel,
        out_shape=[shape(16, 16, 512), shape(16, 16, 512)],
        scratch_shapes=[
            pltpu.VMEM((36, 4, 48, 128), F32),
            pltpu.VMEM((36, 4, 48, 128), F32),
            pltpu.VMEM((36, 4, 48, 128), F32),
            pltpu.VMEM((4, 4, 4, 8, 128), F32),
        ],
        compiler_params=params,
        name="fine",
    )(
        side,
        move(side[:, 8:16], "gy", 1),
        move(side[:, 0:8], "gy", -1),
        coarse,
        move(coarse, "gy", 1),
        move(coarse, "gy", -1),
        inverse,
        center,
    )
    return solution_field, residual


def solution(mesh):
    specs = (P("gx", "gy", None), P("gx", "gy", None))
    return jax.shard_map(shards, mesh=mesh, in_specs=specs, out_specs=specs, check_vma=False)
```

```python
import jax
import jax.numpy as jnp
from jax import lax
from jax.experimental import pallas as pl
from jax.experimental.pallas import tpu as pltpu
from jax.sharding import PartitionSpec as P

CENTER = 8.0 / 3.0
OMEGA = 2.0 / 3.0
SCREEN = 0.05
THIRD = 1.0 - OMEGA
F32 = jnp.float32
HIGH = lax.Precision.HIGHEST


def iota(shape, dim):
    return lax.broadcasted_iota(jnp.int32, shape, dim)


def pairing(rows, columns, factor, value):
    r, c = iota((rows, columns), 0), iota((rows, columns), 1)
    hit = (r // factor == c) if rows > columns else (c // factor == r)
    return jnp.where(hit, value, 0.0).astype(F32)


def stencil_rows(load, rows, blocks):
    v, t = {}, {}
    for x in range(rows[0] - 1, rows[-1] + 2):
        v[x] = load(x, 0)
        t[x] = [a + b for a, b in zip(load(x, -1), load(x, 1))]
    lane = iota(v[rows[0]][0].shape, 1)
    first, last = lane == 0, lane == 127
    zero = jnp.zeros(lane.shape, F32)
    out = {}
    for x in rows:
        m = [t[x - 1][b] + t[x + 1][b] for b in range(blocks)]
        w = [0.5 * m[b] + (t[x][b] + (v[x - 1][b] + v[x + 1][b])) for b in range(blocks)]
        up = [pltpu.roll(w[b], 1, 1) for b in range(blocks)]
        down = [pltpu.roll(w[b], 127, 1) for b in range(blocks)]
        total = []
        for b in range(blocks):
            below = jnp.where(first, up[b - 1] if b else zero, up[b])
            above = jnp.where(last, down[b + 1] if b < blocks - 1 else zero, down[b])
            total.append((below + above) + m[b])
        out[x] = total
    return v, out


def sweep(rows, starts, blocks, source, target, drive, coupling):
    for start in starts:
        def load(x, shift):
            ref, at = source(x)
            return [ref[at, b, pl.ds(start + shift, 8), :] for b in range(blocks)]

        v, out = stencil_rows(load, rows, blocks)
        here = pl.ds(start, 8)
        for x in rows:
            (to, i), (forcing, j), (factor, k) = target(x), drive(x), coupling(x)
            for b in range(blocks):
                to[i, b, here, :] = (
                    THIRD * v[x][b] + factor[k, b, here, :] * out[x][b] + forcing[j, b, here, :]
                )


def in_domain(index, low, count):
    place = low + index - 1
    return jnp.where((place >= 0) & (place < count), 1.0, 0.0).astype(F32)


def place():
    return lax.axis_index("gx"), lax.axis_index("gy"), lax.axis_size("gx"), lax.axis_size("gy")


def restrict_kernel(side_ref, counts_ref, out_ref, first_ref, second_ref, tmp):
    for x in range(8):
        tmp[16 * x : 16 * x + 16, :] = side_ref[2 * x] + side_ref[2 * x + 1]
    halves = pairing(512, 256, 2, 0.5)
    rows = jnp.dot(pairing(64, 128, 2, 1.0), tmp[...], precision=HIGH, preferred_element_type=F32)
    coarse = jnp.dot(rows, halves, precision=HIGH, preferred_element_type=F32)
    for x in range(8):
        out_ref[x] = coarse[8 * x : 8 * x + 8, :]
    out_ref[8] = jnp.zeros((8, 256), F32)
    out_ref[8, 0:4, 0:64] = counts_ref[...].reshape(4, 64).astype(F32)
    first_ref[...] = side_ref[:, 0:8, :]
    second_ref[...] = side_ref[:, 8:16, :]


def coarse_kernel(mid_ref, low_ref, high_ref, c_ref, inv_ref, center_ref, even, odd, drive, coupling):
    gx, gy, n_gx, n_gy = place()
    strips = (low_ref, mid_ref, high_ref)
    counts = jnp.concatenate([strips[j][9 * i + 8][:, 0:64] for i in range(3) for j in range(3)], axis=0)
    spread = jnp.dot(counts, pairing(64, 256, 4, 1.0), precision=HIGH, preferred_element_type=F32)
    weight = OMEGA / (CENTER + (SCREEN * 4.0) * spread)
    sub = iota((8, 128), 0)
    zero = jnp.zeros((8, 128), F32)
    for x in range(26):
        for b in range(2):
            for field in (even, odd):
                for start in (0, 32):
                    field[x, b, start : start + 8, :] = zero
    for i in range(3):
        for j in range(3):
            inside = in_domain(i, gx, n_gx) * in_domain(j, gy, n_gy)
            group = weight[8 * (3 * i + j) : 8 * (3 * i + j) + 8, :] * inside
            here = pl.ds(8 * j + 8, 8)
            for k in range(2):
                for b in range(2):
                    lanes = slice(128 * b, 128 * b + 128)
                    tile = jnp.where(
                        sub < 4,
                        jnp.broadcast_to(group[2 * k : 2 * k + 1, lanes], (8, 128)),
                        jnp.broadcast_to(group[2 * k + 1 : 2 * k + 2, lanes], (8, 128)),
                    )
                    coupling[2 * i + k, b, here, :] = tile * (1.0 / 6.0)
                    for x in range(4):
                        at = 8 * i + 4 * k + x
                        value = tile * strips[j][9 * i + 4 * k + x, :, lanes]
                        drive[at + 1, b, here, :] = value
                        even[at + 1, b, here, :] = value
    for k in range(7):
        halo = 6 - k
        source, target = (even, odd) if k % 2 == 0 else (odd, even)
        starts = (8, 16, 24) if halo > 4 else ((12, 20) if halo else (16,))
        sweep(
            range(-halo, 8 + halo), starts, 2,
            lambda x: (source, x + 9),
            lambda x: (target, x + 9),
            lambda x: (drive, x + 9),
            lambda x: (coupling, (x + 8) // 4),
        )
    for x in range(8):
        c_ref[x] = jnp.concatenate([odd[9 + x, b, 16:24, :] for b in range(2)], axis=1)

    wide = jnp.dot(counts, pairing(64, 512, 8, 1.0), precision=HIGH, preferred_element_type=F32)
    center = CENTER + SCREEN * wide
    inverse = OMEGA / center
    for xb in range(4):
        i, k = ((xb + 1) // 2, (xb + 1) % 2)
        for yb in range(4):
            j, l = ((yb + 1) // 2, (yb + 1) % 2)
            at = 8 * (3 * i + j) + 2 * k + l
            inside = in_domain(i, gx, n_gx) * in_domain(j, gy, n_gy)
            inv_ref[xb, yb : yb + 1, :] = inverse[at : at + 1, :] * inside
            center_ref[xb, yb : yb + 1, :] = center[at : at + 1, :]


def fine_starts(k):
    return (8, 16, 24, 32) if k < 5 else (12, 20, 28)


def inject(rows, targets):
    doubling = pairing(256, 512, 2, 1.0)
    grown = jnp.dot(jnp.concatenate(rows, axis=0), doubling, precision=HIGH, preferred_element_type=F32)
    for n, (field, x, start) in enumerate(targets):
        for b in range(4):
            value = grown[8 * n : 8 * n + 8, 128 * b : 128 * b + 128]
            for dx in range(2):
                for dy in range(2):
                    field[x + dx, b, pl.ds(start + dy, 8, stride=2), :] = value


def weigh(inv_ref, bricks, coupling, first, drive_rows):
    for xb in bricks:
        for yb in range(4):
            here = pl.ds(8 * yb + 8, 8)
            for b in range(4):
                lanes = slice(128 * b, 128 * b + 128)
                tile = jnp.broadcast_to(inv_ref[xb, yb : yb + 1, lanes], (8, 128))
                coupling[xb - first, b, here, :] = tile * (1.0 / 6.0)
                for to, at, sources in drive_rows(xb):
                    ref, x, row = sources[yb]
                    to[at, b, here, :] = tile * ref[x, row : row + 8, lanes]


def inner_kernel(side_ref, side_low, side_high, c_ref, c_low, c_high, inv_ref, even, odd, drive, coupling):
    _, gy, _, n_gy = place()
    zero = jnp.zeros((8, 128), F32)
    for x in range(16):
        for b in range(4):
            odd[x, b, 0:8, :] = zero
            odd[x, b, 40:48, :] = zero
    rows, targets = [], []
    for j, ref in enumerate((c_low, c_ref, c_high)):
        for x in range(8):
            rows.append(ref[x] * in_domain(j, gy, n_gy))
            targets.append((even, 2 * x, 16 * j))
    inject(rows, targets)
    weigh(
        inv_ref, (1, 2), coupling, 1,
        lambda xb: [
            (drive, x, ((side_low, x, 0), (side_ref, x, 0), (side_ref, x, 8), (side_high, x, 0)))
            for x in range(8 * xb - 8, 8 * xb)
        ],
    )
    for k in range(1, 8):
        source, target = (odd, even) if k % 2 == 0 else (even, odd)
        sweep(
            range(k, 16 - k), fine_starts(k), 4,
            lambda x: (source, x),
            lambda x: (target, x),
            lambda x: (drive, x),
            lambda x: (coupling, x // 8),
        )


def outer_kernel(side_ref, side_low, side_high, c_low, c_high, inv_ref, center_ref, inner_even, inner_odd,
                 inner_drive, inner_coupling, solution_ref, residual_ref, even, odd, drive, coupling):
    gx, gy, n_gx, n_gy = place()
    zero = jnp.zeros((8, 128), F32)
    for x in range(36):
        for b in range(4):
            odd[x, b, 0:8, :] = zero
            odd[x, b, 40:48, :] = zero
    rows, targets = [], []
    for i, ref, first in ((0, c_low, 0), (2, c_high, 26)):
        for j in range(3):
            inside = in_domain(i, gx, n_gx) * in_domain(j, gy, n_gy)
            for x in range(5):
                rows.append(ref[x, 8 * j : 8 * j + 8, :] * inside)
                targets.append((even, first + 2 * x, 16 * j))
    inject(rows, targets)
    weigh(
        inv_ref, (0, 3), coupling, 0,
        lambda xb: [
            (drive, x + (2 if xb == 0 else 26), [(side_low if xb == 0 else side_high, x, 8 * yb) for yb in range(4)])
            for x in range(8)
        ],
    )

    def state(k, x):
        if k <= x < 16 - k:
            return (inner_odd if k % 2 else inner_even), x
        return (odd if k % 2 else even), x + 10

    def forcing(x):
        return (inner_drive, x) if 0 <= x < 16 else (drive, x + 10)

    def factor(x):
        return (inner_coupling, x // 8) if 0 <= x < 16 else (coupling, x // 8 + 1)

    for k in range(1, 9):
        for rows in (range(k - 9, k), range(16 - k, 25 - k)):
            sweep(
                rows, fine_starts(k), 4,
                lambda x: state(k - 1, x),
                lambda x: state(k, x),
                forcing,
                factor,
            )
    for start in (16, 24):
        def load(x, shift):
            return [even[x + 10, b, pl.ds(start + shift, 8), :] for b in range(4)]

        v, out = stencil_rows(load, range(16), 4)
        for x in range(16):
            for b in range(4):
                lanes, rows = slice(128 * b, 128 * b + 128), slice(start - 16, start - 8)
                center = center_ref[1 + x // 8, start // 8 - 1 : start // 8, lanes]
                solution_ref[x, rows, lanes] = v[x][b]
                residual_ref[x, rows, lanes] = side_ref[x, rows, lanes] - center * v[x][b] + (1.0 / 6.0) * out[x][b]


def shape(*dims):
    return jax.ShapeDtypeStruct(dims, F32)


def call(kernel, outputs, scratch, name):
    return pl.pallas_call(
        kernel,
        out_shape=[shape(*dims) for dims in outputs],
        scratch_shapes=[pltpu.VMEM(dims, F32) for dims in scratch],
        compiler_params=pltpu.CompilerParams(vmem_limit_bytes=20 * 1024 * 1024),
        name=name,
    )


def shards(right_side, point_counts):
    def move(value, axis, step):
        count = lax.axis_size(axis)
        return lax.ppermute(value, axis, [(i, (i + step) % count) for i in range(count)])

    packed, first, second = call(
        restrict_kernel, [(9, 8, 256), (16, 8, 512), (16, 8, 512)], [(128, 512)], "restrict"
    )(right_side, point_counts)
    packed = jnp.concatenate([move(packed, "gx", 1), packed, move(packed, "gx", -1)], axis=0)
    side_low, side_high = move(second, "gy", 1), move(first, "gy", -1)
    coarse, inverse, center = call(
        coarse_kernel,
        [(8, 8, 256), (4, 4, 512), (4, 4, 512)],
        [(26, 2, 40, 128)] * 3 + [(6, 2, 40, 128)],
        "coarse",
    )(packed, move(packed, "gy", 1), move(packed, "gy", -1))
    coarse_low, coarse_high = move(coarse, "gy", 1), move(coarse, "gy", -1)
    side = jnp.concatenate([side_low, right_side, side_high], axis=1)
    side_left, side_right = move(side[8:16], "gx", 1), move(side[0:8], "gx", -1)
    wide = jnp.concatenate([coarse_low, coarse, coarse_high], axis=1)
    coarse_left, coarse_right = move(wide[3:8], "gx", 1), move(wide[0:5], "gx", -1)
    field = (16, 4, 48, 128)
    inner = call(inner_kernel, [field, field, field, (2, 4, 48, 128)], [], "inner")(
        right_side, side_low, side_high, coarse, coarse_low, coarse_high, inverse
    )
    field = (36, 4, 48, 128)
    return call(
        outer_kernel, [(16, 16, 512)] * 2, [field, field, field, (4, 4, 48, 128)], "outer"
    )(right_side, side_left, side_right, coarse_left, coarse_right, inverse, center, *inner)


def solution(mesh):
    specs = (P("gx", "gy", None), P("gx", "gy", None))
    return jax.shard_map(shards, mesh=mesh, in_specs=specs, out_specs=specs, check_vma=False)
```

```python
import jax
import jax.numpy as jnp
from jax import lax
from jax.experimental import pallas as pl
from jax.experimental.pallas import tpu as pltpu
from jax.sharding import PartitionSpec as P

CENTER = 8.0 / 3.0
OMEGA = 2.0 / 3.0
SCREEN = 0.05
THIRD = 1.0 - OMEGA
F32 = jnp.float32
HIGH = lax.Precision.HIGHEST
COARSE_US = 20
INNER_US = 20


def iota(shape, dim):
    return lax.broadcasted_iota(jnp.int32, shape, dim)


def pairing(rows, columns, factor, value):
    r, c = iota((rows, columns), 0), iota((rows, columns), 1)
    hit = (r // factor == c) if rows > columns else (c // factor == r)
    return jnp.where(hit, value, 0.0).astype(F32)


def stencil_rows(load, rows, blocks):
    v, t = {}, {}
    for x in range(rows[0] - 1, rows[-1] + 2):
        v[x] = load(x, 0)
        t[x] = [a + b for a, b in zip(load(x, -1), load(x, 1))]
    lane = iota(v[rows[0]][0].shape, 1)
    first, last = lane == 0, lane == 127
    zero = jnp.zeros(lane.shape, F32)
    out = {}
    for x in rows:
        m = [t[x - 1][b] + t[x + 1][b] for b in range(blocks)]
        w = [0.5 * m[b] + (t[x][b] + (v[x - 1][b] + v[x + 1][b])) for b in range(blocks)]
        up = [pltpu.roll(w[b], 1, 1) for b in range(blocks)]
        down = [pltpu.roll(w[b], 127, 1) for b in range(blocks)]
        total = []
        for b in range(blocks):
            below = jnp.where(first, up[b - 1] if b else zero, up[b])
            above = jnp.where(last, down[b + 1] if b < blocks - 1 else zero, down[b])
            total.append((below + above) + m[b])
        out[x] = total
    return v, out


def sweep(rows, starts, blocks, source, target, drive, coupling):
    for start in starts:
        def load(x, shift):
            ref, at = source(x)
            return [ref[at, b, pl.ds(start + shift, 8), :] for b in range(blocks)]

        v, out = stencil_rows(load, rows, blocks)
        here = pl.ds(start, 8)
        for x in rows:
            (to, i), (forcing, j), (factor, k) = target(x), drive(x), coupling(x)
            for b in range(blocks):
                to[i, b, here, :] = (
                    THIRD * v[x][b] + factor[k, b, here, :] * out[x][b] + forcing[j, b, here, :]
                )


def in_domain(index, low, count):
    place = low + index - 1
    return jnp.where((place >= 0) & (place < count), 1.0, 0.0).astype(F32)


def place():
    return lax.axis_index("gx"), lax.axis_index("gy"), lax.axis_size("gx"), lax.axis_size("gy")


def restrict_kernel(side_ref, counts_ref, out_ref, first_ref, second_ref, tmp):
    for x in range(8):
        tmp[16 * x : 16 * x + 16, :] = side_ref[2 * x] + side_ref[2 * x + 1]
    halves = pairing(512, 256, 2, 0.5)
    rows = jnp.dot(pairing(64, 128, 2, 1.0), tmp[...], precision=HIGH, preferred_element_type=F32)
    coarse = jnp.dot(rows, halves, precision=HIGH, preferred_element_type=F32)
    for x in range(8):
        out_ref[x] = coarse[8 * x : 8 * x + 8, :]
    out_ref[8] = jnp.zeros((8, 256), F32)
    out_ref[8, 0:4, 0:64] = counts_ref[...].reshape(4, 64).astype(F32)
    first_ref[...] = side_ref[:, 0:8, :]
    second_ref[...] = side_ref[:, 8:16, :]


def coarse_kernel(mid_ref, low_ref, high_ref, c_ref, inv_ref, center_ref, even, odd, drive, coupling):
    gx, gy, n_gx, n_gy = place()
    strips = (low_ref, mid_ref, high_ref)
    counts = jnp.concatenate([strips[j][9 * i + 8][:, 0:64] for i in range(3) for j in range(3)], axis=0)
    spread = jnp.dot(counts, pairing(64, 256, 4, 1.0), precision=HIGH, preferred_element_type=F32)
    weight = OMEGA / (CENTER + (SCREEN * 4.0) * spread)
    sub = iota((8, 128), 0)
    zero = jnp.zeros((8, 128), F32)
    for x in range(26):
        for b in range(2):
            for field in (even, odd):
                for start in (0, 32):
                    field[x, b, start : start + 8, :] = zero
    for i in range(3):
        for j in range(3):
            inside = in_domain(i, gx, n_gx) * in_domain(j, gy, n_gy)
            group = weight[8 * (3 * i + j) : 8 * (3 * i + j) + 8, :] * inside
            here = pl.ds(8 * j + 8, 8)
            for k in range(2):
                for b in range(2):
                    lanes = slice(128 * b, 128 * b + 128)
                    tile = jnp.where(
                        sub < 4,
                        jnp.broadcast_to(group[2 * k : 2 * k + 1, lanes], (8, 128)),
                        jnp.broadcast_to(group[2 * k + 1 : 2 * k + 2, lanes], (8, 128)),
                    )
                    coupling[2 * i + k, b, here, :] = tile * (1.0 / 6.0)
                    for x in range(4):
                        at = 8 * i + 4 * k + x
                        value = tile * strips[j][9 * i + 4 * k + x, :, lanes]
                        drive[at + 1, b, here, :] = value
                        even[at + 1, b, here, :] = value
    for k in range(7):
        halo = 6 - k
        source, target = (even, odd) if k % 2 == 0 else (odd, even)
        starts = (8, 16, 24) if halo > 4 else ((12, 20) if halo else (16,))
        sweep(
            range(-halo, 8 + halo), starts, 2,
            lambda x: (source, x + 9),
            lambda x: (target, x + 9),
            lambda x: (drive, x + 9),
            lambda x: (coupling, (x + 8) // 4),
        )
    for x in range(8):
        c_ref[x] = jnp.concatenate([odd[9 + x, b, 16:24, :] for b in range(2)], axis=1)

    wide = jnp.dot(counts, pairing(64, 512, 8, 1.0), precision=HIGH, preferred_element_type=F32)
    center = CENTER + SCREEN * wide
    inverse = OMEGA / center
    for xb in range(4):
        i, k = ((xb + 1) // 2, (xb + 1) % 2)
        for yb in range(4):
            j, l = ((yb + 1) // 2, (yb + 1) % 2)
            at = 8 * (3 * i + j) + 2 * k + l
            inside = in_domain(i, gx, n_gx) * in_domain(j, gy, n_gy)
            inv_ref[xb, yb : yb + 1, :] = inverse[at : at + 1, :] * inside
            center_ref[xb, yb : yb + 1, :] = center[at : at + 1, :]


def fine_starts(k):
    return (8, 16, 24, 32) if k < 5 else (12, 20, 28)


def inject(rows, targets):
    doubling = pairing(256, 512, 2, 1.0)
    grown = jnp.dot(jnp.concatenate(rows, axis=0), doubling, precision=HIGH, preferred_element_type=F32)
    for n, (field, x, start) in enumerate(targets):
        for b in range(4):
            value = grown[8 * n : 8 * n + 8, 128 * b : 128 * b + 128]
            for dx in range(2):
                for dy in range(2):
                    field[x + dx, b, pl.ds(start + dy, 8, stride=2), :] = value


def weigh(inv_ref, bricks, coupling, first, drive_rows):
    for xb in bricks:
        for yb in range(4):
            here = pl.ds(8 * yb + 8, 8)
            for b in range(4):
                lanes = slice(128 * b, 128 * b + 128)
                tile = jnp.broadcast_to(inv_ref[xb, yb : yb + 1, lanes], (8, 128))
                coupling[xb - first, b, here, :] = tile * (1.0 / 6.0)
                for to, at, sources in drive_rows(xb):
                    ref, x, row = sources[yb]
                    to[at, b, here, :] = tile * ref[x, row : row + 8, lanes]


def inner_kernel(side_ref, side_low, side_high, c_ref, c_low, c_high, inv_ref, even, odd, drive, coupling):
    _, gy, _, n_gy = place()
    zero = jnp.zeros((8, 128), F32)
    for x in range(16):
        for b in range(4):
            odd[x, b, 0:8, :] = zero
            odd[x, b, 40:48, :] = zero
    rows, targets = [], []
    for j, ref in enumerate((c_low, c_ref, c_high)):
        for x in range(8):
            rows.append(ref[x] * in_domain(j, gy, n_gy))
            targets.append((even, 2 * x, 16 * j))
    inject(rows, targets)
    weigh(
        inv_ref, (1, 2), coupling, 1,
        lambda xb: [
            (drive, x, ((side_low, x, 0), (side_ref, x, 0), (side_ref, x, 8), (side_high, x, 0)))
            for x in range(8 * xb - 8, 8 * xb)
        ],
    )
    for k in range(1, 8):
        source, target = (odd, even) if k % 2 == 0 else (even, odd)
        sweep(
            range(k, 16 - k), fine_starts(k), 4,
            lambda x: (source, x),
            lambda x: (target, x),
            lambda x: (drive, x),
            lambda x: (coupling, x // 8),
        )


def outer_kernel(side_ref, side_left, side_right, corner_low, corner_high, c_low, c_high, inv_ref, center_ref,
                 inner_even, inner_odd, inner_drive, inner_coupling, solution_ref, residual_ref,
                 even, odd, drive, coupling):
    gx, gy, n_gx, n_gy = place()
    zero = jnp.zeros((8, 128), F32)
    for x in range(36):
        for b in range(4):
            odd[x, b, 0:8, :] = zero
            odd[x, b, 40:48, :] = zero
    rows, targets = [], []
    for i, ref, first in ((0, c_low, 0), (2, c_high, 26)):
        for j in range(3):
            inside = in_domain(i, gx, n_gx) * in_domain(j, gy, n_gy)
            for x in range(5):
                rows.append(ref[x, 8 * j : 8 * j + 8, :] * inside)
                targets.append((even, first + 2 * x, 16 * j))
    inject(rows, targets)
    def outer_rows(xb):
        first, at, ref = (2, 0, side_left) if xb == 0 else (26, 8, side_right)
        return [
            (drive, x + first, ((corner_low, at + x, 0), (ref, x, 0), (ref, x, 8), (corner_high, at + x, 0)))
            for x in range(8)
        ]

    weigh(inv_ref, (0, 3), coupling, 0, outer_rows)

    def state(k, x):
        if k <= x < 16 - k:
            return (inner_odd if k % 2 else inner_even), x
        return (odd if k % 2 else even), x + 10

    def forcing(x):
        return (inner_drive, x) if 0 <= x < 16 else (drive, x + 10)

    def factor(x):
        return (inner_coupling, x // 8) if 0 <= x < 16 else (coupling, x // 8 + 1)

    for k in range(1, 9):
        for rows in (range(k - 9, k), range(16 - k, 25 - k)):
            sweep(
                rows, fine_starts(k), 4,
                lambda x: state(k - 1, x),
                lambda x: state(k, x),
                forcing,
                factor,
            )
    for start in (16, 24):
        def load(x, shift):
            return [even[x + 10, b, pl.ds(start + shift, 8), :] for b in range(4)]

        v, out = stencil_rows(load, range(16), 4)
        for x in range(16):
            for b in range(4):
                lanes, rows = slice(128 * b, 128 * b + 128), slice(start - 16, start - 8)
                center = center_ref[1 + x // 8, start // 8 - 1 : start // 8, lanes]
                solution_ref[x, rows, lanes] = v[x][b]
                residual_ref[x, rows, lanes] = side_ref[x, rows, lanes] - center * v[x][b] + (1.0 / 6.0) * out[x][b]


def shape(*dims):
    return jax.ShapeDtypeStruct(dims, F32)


def call(kernel, outputs, scratch, name, microseconds):
    cost = pl.CostEstimate(flops=int(microseconds * 1.0e9), bytes_accessed=int(microseconds * 3.69e6), transcendentals=0)
    return pl.pallas_call(
        kernel,
        out_shape=[shape(*dims) for dims in outputs],
        scratch_shapes=[pltpu.VMEM(dims, F32) for dims in scratch],
        compiler_params=pltpu.CompilerParams(vmem_limit_bytes=20 * 1024 * 1024),
        cost_estimate=cost,
        name=name,
    )


def shards(right_side, point_counts):
    def move(value, axis, step):
        count = lax.axis_size(axis)
        return lax.ppermute(value, axis, [(i, (i + step) % count) for i in range(count)])

    packed, first, second = call(
        restrict_kernel, [(9, 8, 256), (16, 8, 512), (16, 8, 512)], [(128, 512)], "restrict", 1
    )(right_side, point_counts)
    packed = jnp.concatenate([move(packed, "gx", 1), packed, move(packed, "gx", -1)], axis=0)
    side_low, side_high = move(second, "gy", 1), move(first, "gy", -1)
    side, side_low, side_high = lax.optimization_barrier((right_side, side_low, side_high))
    side_left, side_right = move(side[8:16], "gx", 1), move(side[0:8], "gx", -1)
    coarse, inverse, center = call(
        coarse_kernel,
        [(8, 8, 256), (4, 4, 512), (4, 4, 512)],
        [(26, 2, 40, 128)] * 3 + [(6, 2, 40, 128)],
        "coarse",
        COARSE_US,
    )(packed, move(packed, "gy", 1), move(packed, "gy", -1))
    coarse, side_left, side_right = lax.optimization_barrier((coarse, side_left, side_right))
    coarse_low, coarse_high = move(coarse, "gy", 1), move(coarse, "gy", -1)
    wide = jnp.concatenate([coarse_low, coarse, coarse_high], axis=1)
    wide, side_left, side_right = lax.optimization_barrier((wide, side_left, side_right))
    coarse_left, coarse_right = move(wide[3:8], "gx", 1), move(wide[0:5], "gx", -1)
    corner_low = move(jnp.concatenate([side_left[:, 8:16], side_right[:, 8:16]], axis=0), "gy", 1)
    corner_high = move(jnp.concatenate([side_left[:, 0:8], side_right[:, 0:8]], axis=0), "gy", -1)
    field = (16, 4, 48, 128)
    inner = call(inner_kernel, [field, field, field, (2, 4, 48, 128)], [], "inner", INNER_US)(
        right_side, side_low, side_high, coarse, coarse_low, coarse_high, inverse
    )
    field = (36, 4, 48, 128)
    return call(
        outer_kernel, [(16, 16, 512)] * 2, [field, field, field, (4, 4, 48, 128)], "outer", 6
    )(
        right_side, side_left, side_right, corner_low, corner_high, coarse_left, coarse_right, inverse, center, *inner
    )


def solution(mesh):
    specs = (P("gx", "gy", None), P("gx", "gy", None))
    return jax.shard_map(shards, mesh=mesh, in_specs=specs, out_specs=specs, check_vma=False)
```

```python
import jax
import jax.numpy as jnp
from jax import lax
from jax.experimental import pallas as pl
from jax.experimental.pallas import tpu as pltpu
from jax.sharding import PartitionSpec as P

CENTER = 8.0 / 3.0
OMEGA = 2.0 / 3.0
SCREEN = 0.05
THIRD = 1.0 - OMEGA
F32 = jnp.float32
HIGH = lax.Precision.HIGHEST
COARSE_US = 20
INNER_US = 20


def iota(shape, dim):
    return lax.broadcasted_iota(jnp.int32, shape, dim)


def pairing(rows, columns, factor, value):
    r, c = iota((rows, columns), 0), iota((rows, columns), 1)
    hit = (r // factor == c) if rows > columns else (c // factor == r)
    return jnp.where(hit, value, 0.0).astype(F32)


def stencil_rows(load, rows, blocks):
    v, t = {}, {}
    for x in range(rows[0] - 1, rows[-1] + 2):
        v[x] = load(x, 0)
        t[x] = [a + b for a, b in zip(load(x, -1), load(x, 1))]
    lane = iota(v[rows[0]][0].shape, 1)
    first, last = lane == 0, lane == 127
    zero = jnp.zeros(lane.shape, F32)
    out = {}
    for x in rows:
        m = [t[x - 1][b] + t[x + 1][b] for b in range(blocks)]
        w = [0.5 * m[b] + (t[x][b] + (v[x - 1][b] + v[x + 1][b])) for b in range(blocks)]
        up = [pltpu.roll(w[b], 1, 1) for b in range(blocks)]
        down = [pltpu.roll(w[b], 127, 1) for b in range(blocks)]
        total = []
        for b in range(blocks):
            below = jnp.where(first, up[b - 1] if b else zero, up[b])
            above = jnp.where(last, down[b + 1] if b < blocks - 1 else zero, down[b])
            total.append((below + above) + m[b])
        out[x] = total
    return v, out


def sweep(rows, starts, blocks, source, target, drive, coupling):
    for start in starts:
        def load(x, shift):
            ref, at = source(x)
            return [ref[at, b, pl.ds(start + shift, 8), :] for b in range(blocks)]

        v, out = stencil_rows(load, rows, blocks)
        here = pl.ds(start, 8)
        for x in rows:
            (to, i), (forcing, j), (factor, k) = target(x), drive(x), coupling(x)
            for b in range(blocks):
                to[i, b, here, :] = (
                    THIRD * v[x][b] + factor[k, b, here, :] * out[x][b] + forcing[j, b, here, :]
                )


def in_domain(index, low, count):
    place = low + index - 1
    return jnp.where((place >= 0) & (place < count), 1.0, 0.0).astype(F32)


def place():
    return lax.axis_index("gx"), lax.axis_index("gy"), lax.axis_size("gx"), lax.axis_size("gy")


def restrict_kernel(side_ref, counts_ref, out_ref, first_ref, last_ref, tmp):
    for x in range(8):
        tmp[16 * x : 16 * x + 16, :] = side_ref[2 * x] + side_ref[2 * x + 1]
    halves = pairing(512, 256, 2, 0.5)
    rows = jnp.dot(pairing(64, 128, 2, 1.0), tmp[...], precision=HIGH, preferred_element_type=F32)
    coarse = jnp.dot(rows, halves, precision=HIGH, preferred_element_type=F32)
    for x in range(8):
        out_ref[x] = coarse[8 * x : 8 * x + 8, :]
    out_ref[8] = jnp.zeros((8, 256), F32)
    out_ref[8, 0:4, 0:64] = counts_ref[...].reshape(4, 64).astype(F32)
    first_ref[...] = side_ref[0:8]
    last_ref[...] = side_ref[8:16]


def coarse_kernel(mid_ref, low_ref, high_ref, c_ref, inv_ref, center_ref, even, odd, drive, coupling):
    gx, gy, n_gx, n_gy = place()
    strips = (low_ref, mid_ref, high_ref)
    counts = jnp.concatenate([strips[j][9 * i + 8][:, 0:64] for i in range(3) for j in range(3)], axis=0)
    spread = jnp.dot(counts, pairing(64, 256, 4, 1.0), precision=HIGH, preferred_element_type=F32)
    weight = OMEGA / (CENTER + (SCREEN * 4.0) * spread)
    sub = iota((8, 128), 0)
    zero = jnp.zeros((8, 128), F32)
    for x in range(26):
        for b in range(2):
            for field in (even, odd):
                for start in (0, 32):
                    field[x, b, start : start + 8, :] = zero
    for i in range(3):
        for j in range(3):
            inside = in_domain(i, gx, n_gx) * in_domain(j, gy, n_gy)
            group = weight[8 * (3 * i + j) : 8 * (3 * i + j) + 8, :] * inside
            here = pl.ds(8 * j + 8, 8)
            for k in range(2):
                for b in range(2):
                    lanes = slice(128 * b, 128 * b + 128)
                    tile = jnp.where(
                        sub < 4,
                        jnp.broadcast_to(group[2 * k : 2 * k + 1, lanes], (8, 128)),
                        jnp.broadcast_to(group[2 * k + 1 : 2 * k + 2, lanes], (8, 128)),
                    )
                    coupling[2 * i + k, b, here, :] = tile * (1.0 / 6.0)
                    for x in range(4):
                        at = 8 * i + 4 * k + x
                        value = tile * strips[j][9 * i + 4 * k + x, :, lanes]
                        drive[at + 1, b, here, :] = value
                        even[at + 1, b, here, :] = value
    for k in range(7):
        halo = 6 - k
        source, target = (even, odd) if k % 2 == 0 else (odd, even)
        starts = (8, 16, 24) if halo > 4 else ((12, 20) if halo else (16,))
        sweep(
            range(-halo, 8 + halo), starts, 2,
            lambda x: (source, x + 9),
            lambda x: (target, x + 9),
            lambda x: (drive, x + 9),
            lambda x: (coupling, (x + 8) // 4),
        )
    for x in range(8):
        c_ref[x] = jnp.concatenate([odd[9 + x, b, 16:24, :] for b in range(2)], axis=1)

    wide = jnp.dot(counts, pairing(64, 512, 8, 1.0), precision=HIGH, preferred_element_type=F32)
    center = CENTER + SCREEN * wide
    inverse = OMEGA / center
    for xb in range(4):
        i, k = ((xb + 1) // 2, (xb + 1) % 2)
        for yb in range(4):
            j, l = ((yb + 1) // 2, (yb + 1) % 2)
            at = 8 * (3 * i + j) + 2 * k + l
            inside = in_domain(i, gx, n_gx) * in_domain(j, gy, n_gy)
            inv_ref[xb, yb : yb + 1, :] = inverse[at : at + 1, :] * inside
            center_ref[xb, yb : yb + 1, :] = center[at : at + 1, :]


def fine_starts(k):
    return (8, 16, 24, 32) if k < 5 else (12, 20, 28)


def inject(rows, targets):
    doubling = pairing(256, 512, 2, 1.0)
    grown = jnp.dot(jnp.concatenate(rows, axis=0), doubling, precision=HIGH, preferred_element_type=F32)
    for n, (field, x, start) in enumerate(targets):
        for b in range(4):
            value = grown[8 * n : 8 * n + 8, 128 * b : 128 * b + 128]
            for dx in range(2):
                for dy in range(2):
                    field[x + dx, b, pl.ds(start + dy, 8, stride=2), :] = value


def weigh(inv_ref, bricks, coupling, first, drive_rows):
    for xb in bricks:
        for yb in range(4):
            here = pl.ds(8 * yb + 8, 8)
            for b in range(4):
                lanes = slice(128 * b, 128 * b + 128)
                tile = jnp.broadcast_to(inv_ref[xb, yb : yb + 1, lanes], (8, 128))
                coupling[xb - first, b, here, :] = tile * (1.0 / 6.0)
                for to, at, sources in drive_rows(xb):
                    ref, x, row = sources[yb]
                    to[at, b, here, :] = tile * ref[x, row : row + 8, lanes]


def inner_kernel(side_ref, side_low, side_high, c_ref, c_low, c_high, inv_ref, even, odd, drive, coupling):
    _, gy, _, n_gy = place()
    zero = jnp.zeros((8, 128), F32)
    for x in range(16):
        for b in range(4):
            odd[x, b, 0:8, :] = zero
            odd[x, b, 40:48, :] = zero
    rows, targets = [], []
    for j, ref in enumerate((c_low, c_ref, c_high)):
        for x in range(8):
            rows.append(ref[x] * in_domain(j, gy, n_gy))
            targets.append((even, 2 * x, 16 * j))
    inject(rows, targets)
    weigh(
        inv_ref, (1, 2), coupling, 1,
        lambda xb: [
            (drive, x, ((side_low, x, 0), (side_ref, x, 0), (side_ref, x, 8), (side_high, x, 0)))
            for x in range(8 * xb - 8, 8 * xb)
        ],
    )
    for k in range(1, 8):
        source, target = (odd, even) if k % 2 == 0 else (even, odd)
        sweep(
            range(k, 16 - k), fine_starts(k), 4,
            lambda x: (source, x),
            lambda x: (target, x),
            lambda x: (drive, x),
            lambda x: (coupling, x // 8),
        )


def outer_kernel(side_ref, side_left, side_right, corner_low, corner_high, c_low, c_high, inv_ref, center_ref,
                 inner_even, inner_odd, inner_drive, inner_coupling, solution_ref, residual_ref,
                 even, odd, drive, coupling):
    gx, gy, n_gx, n_gy = place()
    zero = jnp.zeros((8, 128), F32)
    for x in range(36):
        for b in range(4):
            odd[x, b, 0:8, :] = zero
            odd[x, b, 40:48, :] = zero
    rows, targets = [], []
    for i, ref, first in ((0, c_low, 0), (2, c_high, 26)):
        for j in range(3):
            inside = in_domain(i, gx, n_gx) * in_domain(j, gy, n_gy)
            for x in range(5):
                rows.append(ref[x, 8 * j : 8 * j + 8, :] * inside)
                targets.append((even, first + 2 * x, 16 * j))
    inject(rows, targets)
    def outer_rows(xb):
        first, at, ref = (2, 0, side_left) if xb == 0 else (26, 8, side_right)
        return [
            (drive, x + first, ((corner_low, at + x, 0), (ref, x, 0), (ref, x, 8), (corner_high, at + x, 0)))
            for x in range(8)
        ]

    weigh(inv_ref, (0, 3), coupling, 0, outer_rows)

    def state(k, x):
        if k <= x < 16 - k:
            return (inner_odd if k % 2 else inner_even), x
        return (odd if k % 2 else even), x + 10

    def forcing(x):
        return (inner_drive, x) if 0 <= x < 16 else (drive, x + 10)

    def factor(x):
        return (inner_coupling, x // 8) if 0 <= x < 16 else (coupling, x // 8 + 1)

    for k in range(1, 9):
        for rows in (range(k - 9, k), range(16 - k, 25 - k)):
            sweep(
                rows, fine_starts(k), 4,
                lambda x: state(k - 1, x),
                lambda x: state(k, x),
                forcing,
                factor,
            )
    for start in (16, 24):
        def load(x, shift):
            return [even[x + 10, b, pl.ds(start + shift, 8), :] for b in range(4)]

        v, out = stencil_rows(load, range(16), 4)
        for x in range(16):
            for b in range(4):
                lanes, rows = slice(128 * b, 128 * b + 128), slice(start - 16, start - 8)
                center = center_ref[1 + x // 8, start // 8 - 1 : start // 8, lanes]
                solution_ref[x, rows, lanes] = v[x][b]
                residual_ref[x, rows, lanes] = side_ref[x, rows, lanes] - center * v[x][b] + (1.0 / 6.0) * out[x][b]


def shape(*dims):
    return jax.ShapeDtypeStruct(dims, F32)


def call(kernel, outputs, scratch, name, microseconds):
    cost = pl.CostEstimate(flops=int(microseconds * 1.0e9), bytes_accessed=int(microseconds * 3.69e6), transcendentals=0)
    return pl.pallas_call(
        kernel,
        out_shape=[shape(*dims) for dims in outputs],
        scratch_shapes=[pltpu.VMEM(dims, F32) for dims in scratch],
        compiler_params=pltpu.CompilerParams(vmem_limit_bytes=20 * 1024 * 1024),
        cost_estimate=cost,
        name=name,
    )


def shards(right_side, point_counts):
    def exchange(axis, to_low, to_high):
        count, even = lax.axis_size(axis), lax.axis_index(axis) % 2 == 0
        outer = [(i, (i + (-1 if i % 2 == 0 else 1)) % count) for i in range(count)]
        inner = [(i, i + (1 if i % 2 == 0 else -1)) for i in range(count)]
        same = to_low is to_high
        first = lax.ppermute(to_low if same else jnp.where(even, to_low, to_high), axis, outer)
        second = lax.ppermute(to_low if same else jnp.where(even, to_high, to_low), axis, inner)
        return jnp.where(even, first, second), jnp.where(even, second, first)

    packed, first, last = call(
        restrict_kernel, [(9, 8, 256), (8, 16, 512), (8, 16, 512)], [(128, 512)], "restrict", 1
    )(right_side, point_counts)
    left, right = exchange("gx", packed, packed)
    packed = jnp.concatenate([left, packed, right], axis=0)
    side_left, side_right = exchange("gx", first, last)
    packed, own = lax.optimization_barrier((packed, right_side))
    side_low, side_high = exchange("gy", own[:, 0:8], own[:, 8:16])
    coarse, inverse, center = call(
        coarse_kernel,
        [(8, 8, 256), (4, 4, 512), (4, 4, 512)],
        [(26, 2, 40, 128)] * 3 + [(6, 2, 40, 128)],
        "coarse",
        COARSE_US,
    )(packed, *exchange("gy", packed, packed))
    coarse, side_left, side_right = lax.optimization_barrier((coarse, side_left, side_right))
    coarse_low, coarse_high = exchange("gy", coarse, coarse)
    corner_low, corner_high = exchange(
        "gy",
        jnp.concatenate([side_left[:, 0:8], side_right[:, 0:8]], axis=0),
        jnp.concatenate([side_left[:, 8:16], side_right[:, 8:16]], axis=0),
    )
    wide = jnp.concatenate([coarse_low, coarse, coarse_high], axis=1)
    coarse_left, coarse_right = exchange("gx", wide[0:5], wide[3:8])
    field = (16, 4, 48, 128)
    inner = call(inner_kernel, [field, field, field, (2, 4, 48, 128)], [], "inner", INNER_US)(
        right_side, side_low, side_high, coarse, coarse_low, coarse_high, inverse
    )
    field = (36, 4, 48, 128)
    return call(
        outer_kernel, [(16, 16, 512)] * 2, [field, field, field, (4, 4, 48, 128)], "outer", 6
    )(
        right_side, side_left, side_right, corner_low, corner_high, coarse_left, coarse_right, inverse, center, *inner
    )


def solution(mesh):
    specs = (P("gx", "gy", None), P("gx", "gy", None))
    return jax.shard_map(shards, mesh=mesh, in_specs=specs, out_specs=specs, check_vma=False)
```

```python
import jax
import jax.numpy as jnp
from jax import lax
from jax.experimental import pallas as pl
from jax.experimental.pallas import tpu as pltpu
from jax.sharding import PartitionSpec as P

CENTER = 8.0 / 3.0
OMEGA = 2.0 / 3.0
SCREEN = 0.05
THIRD = 1.0 - OMEGA
F32 = jnp.float32
COARSE_US = 20
INNER_US = 20


def iota(shape, dim):
    return lax.broadcasted_iota(jnp.int32, shape, dim)


def pairing(rows, columns, factor, value):
    r, c = iota((rows, columns), 0), iota((rows, columns), 1)
    hit = (r // factor == c) if rows > columns else (c // factor == r)
    return jnp.where(hit, value, 0.0).astype(F32)


def lanes_from(value, index):
    return jnp.take_along_axis(value, index, axis=1, mode="promise_in_bounds")


def stencil_rows(load, rows, blocks):
    v, t = {}, {}
    for x in range(rows[0] - 1, rows[-1] + 2):
        v[x] = load(x, 0)
        t[x] = [a + b for a, b in zip(load(x, -1), load(x, 1))]
    lane = iota(v[rows[0]][0].shape, 1)
    first, last = lane == 0, lane == 127
    zero = jnp.zeros(lane.shape, F32)
    out = {}
    for x in rows:
        m = [t[x - 1][b] + t[x + 1][b] for b in range(blocks)]
        w = [0.5 * m[b] + (t[x][b] + (v[x - 1][b] + v[x + 1][b])) for b in range(blocks)]
        up = [pltpu.roll(w[b], 1, 1) for b in range(blocks)]
        down = [pltpu.roll(w[b], 127, 1) for b in range(blocks)]
        total = []
        for b in range(blocks):
            below = jnp.where(first, up[b - 1] if b else zero, up[b])
            above = jnp.where(last, down[b + 1] if b < blocks - 1 else zero, down[b])
            total.append((below + above) + m[b])
        out[x] = total
    return v, out


def sweep(rows, starts, blocks, source, target, drive, coupling):
    for start in starts:
        def load(x, shift):
            ref, at = source(x)
            return [ref[at, b, pl.ds(start + shift, 8), :] for b in range(blocks)]

        v, out = stencil_rows(load, rows, blocks)
        here = pl.ds(start, 8)
        for x in rows:
            (to, i), (forcing, j), (factor, k) = target(x), drive(x), coupling(x)
            for b in range(blocks):
                to[i, b, here, :] = (
                    THIRD * v[x][b] + factor[k, b, here, :] * out[x][b] + forcing[j, b, here, :]
                )


def in_domain(index, low, count):
    place = low + index - 1
    return jnp.where((place >= 0) & (place < count), 1.0, 0.0).astype(F32)


def place():
    return lax.axis_index("gx"), lax.axis_index("gy"), lax.axis_size("gx"), lax.axis_size("gy")


def restrict_kernel(side_hbm, counts_hbm, out_ref, first_ref, last_ref, tmp, side_ref, counts_ref, arrived):
    copies = [
        pltpu.make_async_copy(counts_hbm, counts_ref, arrived.at[0]),
        pltpu.make_async_copy(side_hbm, side_ref, arrived.at[1]),
    ]
    for copy in copies:
        copy.start()
    for copy in copies:
        copy.wait()
    lane = iota((8, 128), 1)
    pick = (2 * lane) & 127
    for x in range(8):
        for b in range(4):
            lanes = slice(128 * b, 128 * b + 128)
            for start in (0, 8):
                rows = slice(start, start + 8)
                tmp[b, 16 * x + start : 16 * x + start + 8, :] = (
                    side_ref[2 * x, rows, lanes] + side_ref[2 * x + 1, rows, lanes]
                )
    for x in range(8):
        halves = []
        for b in range(4):
            pair = tmp[b, pl.ds(16 * x, 8, stride=2), :] + tmp[b, pl.ds(16 * x + 1, 8, stride=2), :]
            halves.append(lanes_from(pair + pltpu.roll(pair, 127, 1), pick))
        for b in range(2):
            out_ref[x, :, 128 * b : 128 * b + 128] = 0.5 * jnp.where(lane < 64, halves[2 * b], halves[2 * b + 1])
    out_ref[8] = jnp.zeros((8, 256), F32)
    out_ref[8, 0:4, 0:64] = counts_ref[...].reshape(4, 64).astype(F32)
    first_ref[...] = side_ref[0:8]
    last_ref[...] = side_ref[8:16]


def coarse_kernel(mid_ref, low_ref, high_ref, c_ref, counts_ref, even, odd, drive, coupling):
    gx, gy, n_gx, n_gy = place()
    strips = (low_ref, mid_ref, high_ref)
    counts = jnp.concatenate([strips[j][9 * i + 8][:, 0:64] for i in range(3) for j in range(3)], axis=0)
    counts_ref[:, 0:64] = counts
    spread = jnp.dot(counts, pairing(64, 256, 4, 1.0), preferred_element_type=F32)
    weight = OMEGA / (CENTER + (SCREEN * 4.0) * spread)
    sub = iota((8, 128), 0)
    for i in range(3):
        for j in range(3):
            inside = in_domain(i, gx, n_gx) * in_domain(j, gy, n_gy)
            group = weight[8 * (3 * i + j) : 8 * (3 * i + j) + 8, :] * inside
            here = pl.ds(8 * j + 8, 8)
            for k in range(2):
                for b in range(2):
                    lanes = slice(128 * b, 128 * b + 128)
                    tile = jnp.where(
                        sub < 4,
                        jnp.broadcast_to(group[2 * k : 2 * k + 1, lanes], (8, 128)),
                        jnp.broadcast_to(group[2 * k + 1 : 2 * k + 2, lanes], (8, 128)),
                    )
                    coupling[2 * i + k, b, here, :] = tile * (1.0 / 6.0)
                    for x in range(4):
                        at = 8 * i + 4 * k + x
                        value = tile * strips[j][9 * i + 4 * k + x, :, lanes]
                        drive[at + 1, b, here, :] = value
                        even[at + 1, b, here, :] = value
    for k in range(7):
        halo = 6 - k
        source, target = (even, odd) if k % 2 == 0 else (odd, even)
        starts = (8, 16, 24) if halo > 4 else ((12, 20) if halo else (16,))
        sweep(
            range(-halo, 8 + halo), starts, 2,
            lambda x: (source, x + 9),
            lambda x: (target, x + 9),
            lambda x: (drive, x + 9),
            lambda x: (coupling, (x + 8) // 4),
        )
    for x in range(8):
        c_ref[x] = jnp.concatenate([odd[9 + x, b, 16:24, :] for b in range(2)], axis=1)


def fine_starts(k):
    return (8, 16, 24, 32) if k < 5 else (12, 20, 28)


def inject(value, targets):
    half = iota((8, 128), 1) >> 1
    for b in range(4):
        lanes = 128 * (b // 2)
        grown = lanes_from(value[:, lanes : lanes + 128], half + 64 * (b % 2))
        for field, x, start in targets:
            for dx in range(2):
                for dy in range(2):
                    field[x + dx, b, pl.ds(start + dy, 8, stride=2), :] = grown


def inner_kernel(side_ref, side_low, side_high, c_ref, c_low, c_high, counts_ref,
                 even, odd, drive, coupling, center_ref):
    gx, gy, n_gx, n_gy = place()
    for j, ref in enumerate((c_low, c_ref, c_high)):
        inside = in_domain(j, gy, n_gy)
        for x in range(8):
            inject(ref[x] * inside, [(even, 2 * x, 16 * j)])
    spread = jnp.dot(counts_ref[:, 0:64], pairing(64, 512, 8, 1.0), preferred_element_type=F32)
    center = CENTER + SCREEN * spread
    inverse = OMEGA / center
    for xb in range(4):
        i, k = ((xb + 1) // 2, (xb + 1) % 2)
        for yb in range(4):
            j, l = ((yb + 1) // 2, (yb + 1) % 2)
            at = 8 * (3 * i + j) + 2 * k + l
            scale = inverse[at : at + 1, :] * (in_domain(i, gx, n_gx) * in_domain(j, gy, n_gy))
            center_ref[xb, yb : yb + 1, :] = center[at : at + 1, :]
            here = pl.ds(8 * yb + 8, 8)
            for b in range(4):
                lanes = slice(128 * b, 128 * b + 128)
                tile = jnp.broadcast_to(scale[:, lanes], (8, 128))
                coupling[xb, b, here, :] = tile * (1.0 / 6.0)
                if xb in (1, 2):
                    ref, row = (side_low, side_ref, side_ref, side_high)[yb], (0, 0, 8, 0)[yb]
                    for x in range(8 * xb - 8, 8 * xb):
                        drive[x, b, here, :] = tile * ref[x, row : row + 8, lanes]
    for k in range(1, 8):
        source, target = (odd, even) if k % 2 == 0 else (even, odd)
        sweep(
            range(k, 16 - k), fine_starts(k), 4,
            lambda x: (source, x),
            lambda x: (target, x),
            lambda x: (drive, x),
            lambda x: (coupling, x // 8 + 1),
        )


def outer_kernel(side_ref, side_left, side_right, corner_low, corner_high, c_low, c_high, center_ref,
                 inner_even, inner_odd, inner_drive, coupling, solution_hbm, residual_hbm,
                 even, odd, drive, solution_ref, residual_ref, sent):
    gx, gy, n_gx, n_gy = place()
    for i, ref, first in ((0, c_low, 0), (2, c_high, 26)):
        for j in range(3):
            inside = in_domain(i, gx, n_gx) * in_domain(j, gy, n_gy)
            for x in range(5):
                inject(ref[x, 8 * j : 8 * j + 8, :] * inside, [(even, first + 2 * x, 16 * j)])
    for xb, own, first in ((0, side_left, 0), (3, side_right, 8)):
        for yb in range(4):
            ref, at, row = ((corner_low, first, 0), (own, 0, 0), (own, 0, 8), (corner_high, first, 0))[yb]
            here = pl.ds(8 * yb + 8, 8)
            for b in range(4):
                tile = 6.0 * coupling[xb, b, here, :]
                for x in range(8):
                    drive[first + x, b, here, :] = tile * ref[at + x, row : row + 8, 128 * b : 128 * b + 128]

    def forcing(x):
        return (inner_drive, x) if 0 <= x < 16 else (drive, x + 8 if x < 0 else x - 8)

    def state(k, x):
        if k <= x < 16 - k:
            return (inner_odd if k % 2 else inner_even), x
        return (odd if k % 2 else even), x + 10

    for k in range(1, 9):
        for rows in (range(k - 9, k), range(16 - k, 25 - k)):
            sweep(
                rows, fine_starts(k), 4,
                lambda x: state(k - 1, x),
                lambda x: state(k, x),
                forcing,
                lambda x: (coupling, x // 8 + 1),
            )
    copies = []
    for first in (0, 8):
        for start in (16, 24):
            def load(x, shift):
                return [even[x + 10, b, pl.ds(start + shift, 8), :] for b in range(4)]

            v, out = stencil_rows(load, range(first, first + 8), 4)
            for x in range(first, first + 8):
                for b in range(4):
                    lanes, rows = slice(128 * b, 128 * b + 128), slice(start - 16, start - 8)
                    center = center_ref[1 + x // 8, start // 8 - 1 : start // 8, lanes]
                    solution_ref[x, rows, lanes] = v[x][b]
                    residual_ref[x, rows, lanes] = (
                        side_ref[x, rows, lanes] - center * v[x][b] + (1.0 / 6.0) * out[x][b]
                    )
        part = pl.ds(first, 8)
        for n, (source, target) in enumerate(((solution_ref, solution_hbm), (residual_ref, residual_hbm))):
            copies.append(pltpu.make_async_copy(source.at[part], target.at[part], sent.at[first // 4 + n]))
            copies[-1].start()
    for copy in copies:
        copy.wait()


def shape(*dims):
    return jax.ShapeDtypeStruct(dims, F32)


def call(kernel, outputs, scratch, name, microseconds, **specs):
    cost = pl.CostEstimate(flops=int(microseconds * 1.0e9), bytes_accessed=int(microseconds * 3.69e6), transcendentals=0)
    return pl.pallas_call(
        kernel,
        out_shape=[shape(*dims) for dims in outputs],
        scratch_shapes=[pltpu.VMEM(dims, F32) if isinstance(dims, tuple) else dims for dims in scratch],
        compiler_params=pltpu.CompilerParams(vmem_limit_bytes=20 * 1024 * 1024),
        cost_estimate=cost,
        name=name,
        **specs,
    )


def shards(right_side, point_counts):
    def exchange(axis, to_low, to_high):
        count, even = lax.axis_size(axis), lax.axis_index(axis) % 2 == 0
        outer = [(i, (i + (-1 if i % 2 == 0 else 1)) % count) for i in range(count)]
        inner = [(i, i + (1 if i % 2 == 0 else -1)) for i in range(count)]
        same = to_low is to_high
        first = lax.ppermute(to_low if same else jnp.where(even, to_low, to_high), axis, outer)
        second = lax.ppermute(to_low if same else jnp.where(even, to_high, to_low), axis, inner)
        return jnp.where(even, first, second), jnp.where(even, second, first)

    packed, first, last = call(
        restrict_kernel,
        [(9, 8, 256), (8, 16, 512), (8, 16, 512)],
        [(4, 128, 128), (16, 16, 512), pltpu.VMEM((2, 2, 64), jnp.int32), pltpu.SemaphoreType.DMA((2,))],
        "restrict",
        1,
        in_specs=[pl.BlockSpec(memory_space=pltpu.MemorySpace.HBM)] * 2,
    )(
        pltpu.with_memory_space_constraint(right_side, pltpu.MemorySpace.HBM),
        pltpu.with_memory_space_constraint(point_counts, pltpu.MemorySpace.HBM),
    )
    left, right = exchange("gx", packed, packed)
    packed = jnp.concatenate([left, packed, right], axis=0)
    side_left, side_right = exchange("gx", first, last)
    packed, own = lax.optimization_barrier((packed, right_side))
    side_low, side_high = exchange("gy", own[:, 0:8], own[:, 8:16])
    coarse, counts = call(
        coarse_kernel,
        [(8, 8, 256), (72, 128)],
        [(26, 2, 40, 128)] * 3 + [(6, 2, 40, 128)],
        "coarse",
        COARSE_US,
    )(packed, *exchange("gy", packed, packed))
    coarse, side_left, side_right = lax.optimization_barrier((coarse, side_left, side_right))
    coarse_low, coarse_high = exchange("gy", coarse, coarse)
    corner_low, corner_high = exchange(
        "gy",
        jnp.concatenate([side_left[:, 0:8], side_right[:, 0:8]], axis=0),
        jnp.concatenate([side_left[:, 8:16], side_right[:, 8:16]], axis=0),
    )
    wide = jnp.concatenate([coarse_low, coarse, coarse_high], axis=1)
    coarse_left, coarse_right = exchange("gx", wide[0:5], wide[3:8])
    field = (16, 4, 48, 128)
    even, odd, drive, coupling, center = call(
        inner_kernel, [field, field, field, (4, 4, 48, 128), (4, 4, 512)], [], "inner", INNER_US
    )(
        right_side, side_low, side_high, coarse, coarse_low, coarse_high, counts
    )
    field, block = (36, 4, 48, 128), (16, 16, 512)
    return call(
        outer_kernel,
        [block, block],
        [field, field, (16, 4, 48, 128), block, block, pltpu.SemaphoreType.DMA((4,))],
        "outer",
        6,
        out_specs=[pl.BlockSpec(memory_space=pltpu.MemorySpace.HBM)] * 2,
    )(
        right_side, side_left, side_right, corner_low, corner_high, coarse_left, coarse_right, center,
        even, odd, drive, coupling,
    )


def solution(mesh):
    specs = (P("gx", "gy", None), P("gx", "gy", None))
    return jax.shard_map(shards, mesh=mesh, in_specs=specs, out_specs=specs, check_vma=False)
```

```python
import jax
import jax.numpy as jnp
from jax import lax
from jax.experimental import pallas as pl
from jax.experimental.pallas import tpu as pltpu
from jax.sharding import PartitionSpec as P

CENTER = 8.0 / 3.0
OMEGA = 2.0 / 3.0
SCREEN = 0.05
THIRD = 1.0 - OMEGA
F32 = jnp.float32
COARSE_US = 20
INNER_US = 20


def iota(shape, dim):
    return lax.broadcasted_iota(jnp.int32, shape, dim)


def pairing(rows, columns, factor, value):
    r, c = iota((rows, columns), 0), iota((rows, columns), 1)
    hit = (r // factor == c) if rows > columns else (c // factor == r)
    return jnp.where(hit, value, 0.0).astype(F32)


def lanes_from(value, index):
    return jnp.take_along_axis(value, index, axis=1, mode="promise_in_bounds")


def stencil_rows(load, rows, blocks):
    v, t = {}, {}
    for x in range(rows[0] - 1, rows[-1] + 2):
        v[x] = load(x, 0)
        t[x] = [a + b for a, b in zip(load(x, -1), load(x, 1))]
    lane = iota(v[rows[0]][0].shape, 1)
    first, last = lane == 0, lane == 127
    zero = jnp.zeros(lane.shape, F32)
    out = {}
    for x in rows:
        m = [t[x - 1][b] + t[x + 1][b] for b in range(blocks)]
        w = [0.5 * m[b] + (t[x][b] + (v[x - 1][b] + v[x + 1][b])) for b in range(blocks)]
        up = [pltpu.roll(w[b], 1, 1) for b in range(blocks)]
        down = [pltpu.roll(w[b], 127, 1) for b in range(blocks)]
        total = []
        for b in range(blocks):
            below = jnp.where(first, up[b - 1] if b else zero, up[b])
            above = jnp.where(last, down[b + 1] if b < blocks - 1 else zero, down[b])
            total.append((below + above) + m[b])
        out[x] = total
    return v, out


def sweep(rows, starts, blocks, source, target, drive, coupling):
    for start in starts:
        def load(x, shift):
            ref, at = source(x)
            return [ref[at, b, pl.ds(start + shift, 8), :] for b in range(blocks)]

        v, out = stencil_rows(load, rows, blocks)
        here = pl.ds(start, 8)
        for x in rows:
            (to, i), (forcing, j), (factor, k) = target(x), drive(x), coupling(x)
            for b in range(blocks):
                to[i, b, here, :] = (
                    THIRD * v[x][b] + factor[k, b, here, :] * out[x][b] + forcing[j, b, here, :]
                )


def in_domain(index, low, count):
    place = low + index - 1
    return jnp.where((place >= 0) & (place < count), 1.0, 0.0).astype(F32)


def place():
    return lax.axis_index("gx"), lax.axis_index("gy"), lax.axis_size("gx"), lax.axis_size("gy")


def restrict_kernel(side_hbm, counts_hbm, out_ref, first_ref, last_ref, tmp, side_ref, counts_ref, arrived):
    copies = [
        pltpu.make_async_copy(counts_hbm, counts_ref, arrived.at[0]),
        pltpu.make_async_copy(side_hbm.at[0:8], side_ref.at[0:8], arrived.at[1]),
        pltpu.make_async_copy(side_hbm.at[8:16], side_ref.at[8:16], arrived.at[2]),
    ]
    for copy in copies:
        copy.start()
    lane = iota((8, 128), 1)
    pick = (2 * lane) & 127
    for part in range(2):
        copies[1 + part].wait()
        for x in range(4 * part, 4 * part + 4):
            for b in range(4):
                lanes = slice(128 * b, 128 * b + 128)
                for start in (0, 8):
                    rows = slice(start, start + 8)
                    tmp[b, 16 * x + start : 16 * x + start + 8, :] = (
                        side_ref[2 * x, rows, lanes] + side_ref[2 * x + 1, rows, lanes]
                    )
        for x in range(4 * part, 4 * part + 4):
            halves = []
            for b in range(4):
                pair = tmp[b, pl.ds(16 * x, 8, stride=2), :] + tmp[b, pl.ds(16 * x + 1, 8, stride=2), :]
                halves.append(lanes_from(pair + pltpu.roll(pair, 127, 1), pick))
            for b in range(2):
                out_ref[x, :, 128 * b : 128 * b + 128] = 0.5 * jnp.where(
                    lane < 64, halves[2 * b], halves[2 * b + 1]
                )
        (first_ref, last_ref)[part][...] = side_ref[8 * part : 8 * part + 8]
    copies[0].wait()
    out_ref[8] = jnp.zeros((8, 256), F32)
    out_ref[8, 0:4, 0:64] = counts_ref[...].reshape(4, 64).astype(F32)


def coarse_kernel(mid_ref, low_ref, high_ref, c_ref, counts_ref, even, odd, drive, coupling):
    gx, gy, n_gx, n_gy = place()
    strips = (low_ref, mid_ref, high_ref)
    counts = jnp.concatenate([strips[j][row][:, 0:64] for row in (7, 16, 24) for j in range(3)], axis=0)
    counts_ref[:, 0:64] = counts
    spread = jnp.dot(counts, pairing(64, 256, 4, 1.0), preferred_element_type=F32)
    weight = OMEGA / (CENTER + (SCREEN * 4.0) * spread)
    sub = iota((8, 128), 0)
    for i in range(3):
        for j in range(3):
            inside = in_domain(i, gx, n_gx) * in_domain(j, gy, n_gy)
            group = weight[8 * (3 * i + j) : 8 * (3 * i + j) + 8, :] * inside
            here = pl.ds(8 * j + 8, 8)
            for k in range(2):
                for b in range(2):
                    lanes = slice(128 * b, 128 * b + 128)
                    tile = jnp.where(
                        sub < 4,
                        jnp.broadcast_to(group[2 * k : 2 * k + 1, lanes], (8, 128)),
                        jnp.broadcast_to(group[2 * k + 1 : 2 * k + 2, lanes], (8, 128)),
                    )
                    coupling[2 * i + k, b, here, :] = tile * (1.0 / 6.0)
                    for x in range(4):
                        at = 8 * i + 4 * k + x
                        if at in (0, 23):
                            continue
                        value = tile * strips[j][at + i - 1, :, lanes]
                        drive[at + 1, b, here, :] = value
                        even[at + 1, b, here, :] = value
    for k in range(7):
        halo = 6 - k
        source, target = (even, odd) if k % 2 == 0 else (odd, even)
        starts = (8, 16, 24) if halo > 4 else ((12, 20) if halo else (16,))
        sweep(
            range(-halo, 8 + halo), starts, 2,
            lambda x: (source, x + 9),
            lambda x: (target, x + 9),
            lambda x: (drive, x + 9),
            lambda x: (coupling, (x + 8) // 4),
        )
    for x in range(8):
        c_ref[x] = jnp.concatenate([odd[9 + x, b, 16:24, :] for b in range(2)], axis=1)


def fine_starts(k):
    return (8, 16, 24, 32) if k < 5 else (12, 20, 28)


def inject(value, targets):
    half = iota((8, 128), 1) >> 1
    for b in range(4):
        lanes = 128 * (b // 2)
        grown = lanes_from(value[:, lanes : lanes + 128], half + 64 * (b % 2))
        for field, x, start in targets:
            for dx in range(2):
                for dy in range(2):
                    field[x + dx, b, pl.ds(start + dy, 8, stride=2), :] = grown


def inner_kernel(side_ref, side_low, side_high, c_ref, c_low, c_high, counts_ref,
                 even, odd, drive, coupling, center_ref):
    gx, gy, n_gx, n_gy = place()
    for j, ref in enumerate((c_low, c_ref, c_high)):
        inside = in_domain(j, gy, n_gy)
        for x in range(8):
            inject(ref[x] * inside, [(even, 2 * x, 16 * j)])
    spread = jnp.dot(counts_ref[:, 0:64], pairing(64, 512, 8, 1.0), preferred_element_type=F32)
    center = CENTER + SCREEN * spread
    inverse = OMEGA / center
    for xb in range(4):
        i, k = ((xb + 1) // 2, (xb + 1) % 2)
        for yb in range(4):
            j, l = ((yb + 1) // 2, (yb + 1) % 2)
            at = 8 * (3 * i + j) + 2 * k + l
            scale = inverse[at : at + 1, :] * (in_domain(i, gx, n_gx) * in_domain(j, gy, n_gy))
            center_ref[xb, yb : yb + 1, :] = center[at : at + 1, :]
            here = pl.ds(8 * yb + 8, 8)
            for b in range(4):
                lanes = slice(128 * b, 128 * b + 128)
                tile = jnp.broadcast_to(scale[:, lanes], (8, 128))
                coupling[xb, b, here, :] = tile * (1.0 / 6.0)
                if xb in (1, 2):
                    ref, row = (side_low, side_ref, side_ref, side_high)[yb], (0, 0, 8, 0)[yb]
                    for x in range(8 * xb - 8, 8 * xb):
                        drive[x, b, here, :] = tile * ref[x, row : row + 8, lanes]
    for k in range(1, 8):
        source, target = (odd, even) if k % 2 == 0 else (even, odd)
        sweep(
            range(k, 16 - k), fine_starts(k), 4,
            lambda x: (source, x),
            lambda x: (target, x),
            lambda x: (drive, x),
            lambda x: (coupling, x // 8 + 1),
        )


def outer_kernel(side_ref, side_left, side_right, corner_low, corner_high, c_low, c_high, center_ref,
                 inner_even, inner_odd, inner_drive, coupling, solution_hbm, residual_hbm,
                 even, odd, drive, solution_ref, residual_ref, sent):
    gx, gy, n_gx, n_gy = place()
    for i, ref, first in ((0, c_low, 0), (2, c_high, 26)):
        for j in range(3):
            inside = in_domain(i, gx, n_gx) * in_domain(j, gy, n_gy)
            for x in range(5):
                inject(ref[x, 8 * j : 8 * j + 8, :] * inside, [(even, first + 2 * x, 16 * j)])
    for xb, own, first in ((0, side_left, 0), (3, side_right, 8)):
        for yb in range(4):
            ref, at, row = ((corner_low, first, 0), (own, 0, 0), (own, 0, 8), (corner_high, first, 0))[yb]
            here = pl.ds(8 * yb + 8, 8)
            for b in range(4):
                tile = 6.0 * coupling[xb, b, here, :]
                for x in range(8):
                    drive[first + x, b, here, :] = tile * ref[at + x, row : row + 8, 128 * b : 128 * b + 128]

    def forcing(x):
        return (inner_drive, x) if 0 <= x < 16 else (drive, x + 8 if x < 0 else x - 8)

    def state(k, x):
        if k <= x < 16 - k:
            return (inner_odd if k % 2 else inner_even), x
        return (odd if k % 2 else even), x + 10

    for k in range(1, 9):
        for rows in (range(k - 9, k), range(16 - k, 25 - k)) if k < 8 else (range(-1, 17),):
            sweep(
                rows, fine_starts(k), 4,
                lambda x: state(k - 1, x),
                lambda x: state(k, x),
                forcing,
                lambda x: (coupling, x // 8 + 1),
            )
    copies = []
    for first in (0, 4, 8, 12):
        for start in (16, 24):
            def load(x, shift):
                return [even[x + 10, b, pl.ds(start + shift, 8), :] for b in range(4)]

            v, out = stencil_rows(load, range(first, first + 4), 4)
            for x in range(first, first + 4):
                for b in range(4):
                    lanes, rows = slice(128 * b, 128 * b + 128), slice(start - 16, start - 8)
                    center = center_ref[1 + x // 8, start // 8 - 1 : start // 8, lanes]
                    solution_ref[x, rows, lanes] = v[x][b]
                    residual_ref[x, rows, lanes] = (
                        side_ref[x, rows, lanes] - center * v[x][b] + (1.0 / 6.0) * out[x][b]
                    )
        part = pl.ds(first, 4)
        for n, (source, target) in enumerate(((solution_ref, solution_hbm), (residual_ref, residual_hbm))):
            copies.append(pltpu.make_async_copy(source.at[part], target.at[part], sent.at[first // 2 + n]))
            copies[-1].start()
    for copy in copies:
        copy.wait()


def shape(*dims):
    return jax.ShapeDtypeStruct(dims, F32)


def call(kernel, outputs, scratch, name, microseconds, **specs):
    cost = pl.CostEstimate(flops=int(microseconds * 1.0e9), bytes_accessed=int(microseconds * 3.69e6), transcendentals=0)
    return pl.pallas_call(
        kernel,
        out_shape=[shape(*dims) for dims in outputs],
        scratch_shapes=[pltpu.VMEM(dims, F32) if isinstance(dims, tuple) else dims for dims in scratch],
        compiler_params=pltpu.CompilerParams(vmem_limit_bytes=20 * 1024 * 1024),
        cost_estimate=cost,
        name=name,
        **specs,
    )


def shards(right_side, point_counts):
    def exchange(axis, to_low, to_high):
        count, even = lax.axis_size(axis), lax.axis_index(axis) % 2 == 0
        outer = [(i, (i + (-1 if i % 2 == 0 else 1)) % count) for i in range(count)]
        inner = [(i, i + (1 if i % 2 == 0 else -1)) for i in range(count)]
        same = to_low is to_high
        first = lax.ppermute(to_low if same else jnp.where(even, to_low, to_high), axis, outer)
        second = lax.ppermute(to_low if same else jnp.where(even, to_high, to_low), axis, inner)
        return jnp.where(even, first, second), jnp.where(even, second, first)

    packed, first, last = call(
        restrict_kernel,
        [(9, 8, 256), (8, 16, 512), (8, 16, 512)],
        [(4, 128, 128), (16, 16, 512), pltpu.VMEM((2, 2, 64), jnp.int32), pltpu.SemaphoreType.DMA((3,))],
        "restrict",
        1,
        in_specs=[pl.BlockSpec(memory_space=pltpu.MemorySpace.HBM)] * 2,
    )(
        pltpu.with_memory_space_constraint(right_side, pltpu.MemorySpace.HBM),
        pltpu.with_memory_space_constraint(point_counts, pltpu.MemorySpace.HBM),
    )
    left, right = exchange("gx", packed, packed)
    packed = jnp.concatenate([left[1:9], packed, right[0:7], right[8:9]], axis=0)
    side_left, side_right = exchange("gx", first, last)
    packed, own = lax.optimization_barrier((packed, right_side))
    side_low, side_high = exchange("gy", own[:, 0:8], own[:, 8:16])
    coarse, counts = call(
        coarse_kernel,
        [(8, 8, 256), (72, 128)],
        [(26, 2, 40, 128)] * 3 + [(6, 2, 40, 128)],
        "coarse",
        COARSE_US,
    )(packed, *exchange("gy", packed, packed))
    coarse, side_left, side_right = lax.optimization_barrier((coarse, side_left, side_right))
    coarse_low, coarse_high = exchange("gy", coarse, coarse)
    corner_low, corner_high = exchange(
        "gy",
        jnp.concatenate([side_left[:, 0:8], side_right[:, 0:8]], axis=0),
        jnp.concatenate([side_left[:, 8:16], side_right[:, 8:16]], axis=0),
    )
    wide = jnp.concatenate([coarse_low, coarse, coarse_high], axis=1)
    coarse_left, coarse_right = exchange("gx", wide[0:5], wide[3:8])
    field = (16, 4, 48, 128)
    even, odd, drive, coupling, center = call(
        inner_kernel, [field, field, field, (4, 4, 48, 128), (4, 4, 512)], [], "inner", INNER_US
    )(
        right_side, side_low, side_high, coarse, coarse_low, coarse_high, counts
    )
    field, block = (36, 4, 48, 128), (16, 16, 512)
    return call(
        outer_kernel,
        [block, block],
        [field, field, (16, 4, 48, 128), block, block, pltpu.SemaphoreType.DMA((8,))],
        "outer",
        6,
        out_specs=[pl.BlockSpec(memory_space=pltpu.MemorySpace.HBM)] * 2,
    )(
        right_side, side_left, side_right, corner_low, corner_high, coarse_left, coarse_right, center,
        even, odd, drive, coupling,
    )


def solution(mesh):
    specs = (P("gx", "gy", None), P("gx", "gy", None))
    return jax.shard_map(shards, mesh=mesh, in_specs=specs, out_specs=specs, check_vma=False)
```

```python
import jax
import jax.numpy as jnp
from jax import lax
from jax.experimental import pallas as pl
from jax.experimental.pallas import tpu as pltpu
from jax.sharding import PartitionSpec as P

CENTER = 8.0 / 3.0
OMEGA = 2.0 / 3.0
SCREEN = 0.05
THIRD = 1.0 - OMEGA
F32 = jnp.float32
COARSE_US = 20
INNER_US = 20


def iota(shape, dim):
    return lax.broadcasted_iota(jnp.int32, shape, dim)


def pairing(rows, columns, factor, value):
    r, c = iota((rows, columns), 0), iota((rows, columns), 1)
    hit = (r // factor == c) if rows > columns else (c // factor == r)
    return jnp.where(hit, value, 0.0).astype(F32)


def lanes_from(value, index):
    return jnp.take_along_axis(value, index, axis=1, mode="promise_in_bounds")


def stencil_rows(load, rows, blocks):
    v, t = {}, {}
    for x in range(rows[0] - 1, rows[-1] + 2):
        v[x] = load(x, 0)
        t[x] = [a + b for a, b in zip(load(x, -1), load(x, 1))]
    lane = iota(v[rows[0]][0].shape, 1)
    first, last = lane == 0, lane == 127
    zero = jnp.zeros(lane.shape, F32)
    out = {}
    for x in rows:
        m = [t[x - 1][b] + t[x + 1][b] for b in range(blocks)]
        w = [0.5 * m[b] + (t[x][b] + (v[x - 1][b] + v[x + 1][b])) for b in range(blocks)]
        up = [pltpu.roll(w[b], 1, 1) for b in range(blocks)]
        down = [pltpu.roll(w[b], 127, 1) for b in range(blocks)]
        total = []
        for b in range(blocks):
            below = jnp.where(first, up[b - 1] if b else zero, up[b])
            above = jnp.where(last, down[b + 1] if b < blocks - 1 else zero, down[b])
            total.append((below + above) + m[b])
        out[x] = total
    return v, out


def sweep(rows, starts, blocks, source, target, drive, coupling):
    for start in starts:
        def load(x, shift):
            ref, at = source(x)
            return [ref[at, b, pl.ds(start + shift, 8), :] for b in range(blocks)]

        v, out = stencil_rows(load, rows, blocks)
        here = pl.ds(start, 8)
        for x in rows:
            (to, i), (forcing, j), (factor, k) = target(x), drive(x), coupling(x)
            for b in range(blocks):
                to[i, b, here, :] = (
                    THIRD * v[x][b] + factor[k, b, here, :] * out[x][b] + forcing[j, b, here, :]
                )


def in_domain(index, low, count):
    place = low + index - 1
    return jnp.where((place >= 0) & (place < count), 1.0, 0.0).astype(F32)


def place():
    return lax.axis_index("gx"), lax.axis_index("gy"), lax.axis_size("gx"), lax.axis_size("gy")


def restrict_kernel(side_hbm, counts_hbm, out_ref, tmp, side_ref, counts_ref, arrived):
    copies = [
        pltpu.make_async_copy(counts_hbm, counts_ref, arrived.at[0]),
        pltpu.make_async_copy(side_hbm, side_ref, arrived.at[1]),
    ]
    for copy in copies:
        copy.start()
    for copy in copies:
        copy.wait()
    lane = iota((8, 128), 1)
    pick = (2 * lane) & 127
    for x in range(8):
        for b in range(4):
            lanes = slice(128 * b, 128 * b + 128)
            for start in (0, 8):
                rows = slice(start, start + 8)
                tmp[b, 16 * x + start : 16 * x + start + 8, :] = (
                    side_ref[2 * x, rows, lanes] + side_ref[2 * x + 1, rows, lanes]
                )
    for x in range(8):
        halves = []
        for b in range(4):
            pair = tmp[b, pl.ds(16 * x, 8, stride=2), :] + tmp[b, pl.ds(16 * x + 1, 8, stride=2), :]
            halves.append(lanes_from(pair + pltpu.roll(pair, 127, 1), pick))
        for b in range(2):
            out_ref[x, :, 128 * b : 128 * b + 128] = 0.5 * jnp.where(lane < 64, halves[2 * b], halves[2 * b + 1])
    out_ref[8] = jnp.zeros((8, 256), F32)
    out_ref[8, 0:4, 0:64] = counts_ref[...].reshape(4, 64).astype(F32)


def slices_kernel(packed_ref, side_ref, first_ref, last_ref):
    first_ref[...] = side_ref[0:8]
    last_ref[...] = side_ref[8:16]


def coarse_kernel(mid_ref, low_ref, high_ref, c_ref, counts_ref, even, odd, drive, coupling):
    gx, gy, n_gx, n_gy = place()
    strips = (low_ref, mid_ref, high_ref)
    counts = jnp.concatenate([strips[j][9 * i + 8][:, 0:64] for i in range(3) for j in range(3)], axis=0)
    counts_ref[:, 0:64] = counts
    spread = jnp.dot(counts, pairing(64, 256, 4, 1.0), preferred_element_type=F32)
    weight = OMEGA / (CENTER + (SCREEN * 4.0) * spread)
    sub = iota((8, 128), 0)
    for i in range(3):
        for j in range(3):
            inside = in_domain(i, gx, n_gx) * in_domain(j, gy, n_gy)
            group = weight[8 * (3 * i + j) : 8 * (3 * i + j) + 8, :] * inside
            here = pl.ds(8 * j + 8, 8)
            for k in range(2):
                for b in range(2):
                    lanes = slice(128 * b, 128 * b + 128)
                    tile = jnp.where(
                        sub < 4,
                        jnp.broadcast_to(group[2 * k : 2 * k + 1, lanes], (8, 128)),
                        jnp.broadcast_to(group[2 * k + 1 : 2 * k + 2, lanes], (8, 128)),
                    )
                    coupling[2 * i + k, b, here, :] = tile * (1.0 / 6.0)
                    for x in range(4):
                        at = 8 * i + 4 * k + x
                        value = tile * strips[j][9 * i + 4 * k + x, :, lanes]
                        drive[at + 1, b, here, :] = value
                        even[at + 1, b, here, :] = value
    for k in range(7):
        halo = 6 - k
        source, target = (even, odd) if k % 2 == 0 else (odd, even)
        starts = (8, 16, 24) if halo > 4 else ((12, 20) if halo else (16,))
        sweep(
            range(-halo, 8 + halo), starts, 2,
            lambda x: (source, x + 9),
            lambda x: (target, x + 9),
            lambda x: (drive, x + 9),
            lambda x: (coupling, (x + 8) // 4),
        )
    for x in range(8):
        c_ref[x] = jnp.concatenate([odd[9 + x, b, 16:24, :] for b in range(2)], axis=1)


def fine_starts(k):
    return (8, 16, 24, 32) if k < 5 else (12, 20, 28)


def inject(value, targets):
    half = iota((8, 128), 1) >> 1
    for b in range(4):
        lanes = 128 * (b // 2)
        grown = lanes_from(value[:, lanes : lanes + 128], half + 64 * (b % 2))
        for field, x, start in targets:
            for dx in range(2):
                for dy in range(2):
                    field[x + dx, b, pl.ds(start + dy, 8, stride=2), :] = grown


def inner_kernel(side_ref, side_low, side_high, c_ref, c_low, c_high, counts_ref,
                 even, odd, drive, coupling, center_ref):
    gx, gy, n_gx, n_gy = place()
    for j, ref in enumerate((c_low, c_ref, c_high)):
        inside = in_domain(j, gy, n_gy)
        for x in range(8):
            inject(ref[x] * inside, [(even, 2 * x, 16 * j)])
    spread = jnp.dot(counts_ref[:, 0:64], pairing(64, 512, 8, 1.0), preferred_element_type=F32)
    center = CENTER + SCREEN * spread
    inverse = OMEGA / center
    for xb in range(4):
        i, k = ((xb + 1) // 2, (xb + 1) % 2)
        for yb in range(4):
            j, l = ((yb + 1) // 2, (yb + 1) % 2)
            at = 8 * (3 * i + j) + 2 * k + l
            scale = inverse[at : at + 1, :] * (in_domain(i, gx, n_gx) * in_domain(j, gy, n_gy))
            center_ref[xb, yb : yb + 1, :] = center[at : at + 1, :]
            here = pl.ds(8 * yb + 8, 8)
            for b in range(4):
                lanes = slice(128 * b, 128 * b + 128)
                tile = jnp.broadcast_to(scale[:, lanes], (8, 128))
                coupling[xb, b, here, :] = tile * (1.0 / 6.0)
                if xb in (1, 2):
                    ref, row = (side_low, side_ref, side_ref, side_high)[yb], (0, 0, 8, 0)[yb]
                    for x in range(8 * xb - 8, 8 * xb):
                        drive[x, b, here, :] = tile * ref[x, row : row + 8, lanes]
    for k in range(1, 8):
        source, target = (odd, even) if k % 2 == 0 else (even, odd)
        sweep(
            range(k, 16 - k), fine_starts(k), 4,
            lambda x: (source, x),
            lambda x: (target, x),
            lambda x: (drive, x),
            lambda x: (coupling, x // 8 + 1),
        )


def outer_kernel(side_ref, side_left, side_right, corner_low, corner_high, c_low, c_high, center_ref,
                 inner_even, inner_odd, inner_drive, coupling, solution_hbm, residual_hbm,
                 even, odd, drive, solution_ref, residual_ref, sent):
    gx, gy, n_gx, n_gy = place()
    for i, ref, first in ((0, c_low, 0), (2, c_high, 26)):
        for j in range(3):
            inside = in_domain(i, gx, n_gx) * in_domain(j, gy, n_gy)
            for x in range(5):
                inject(ref[x, 8 * j : 8 * j + 8, :] * inside, [(even, first + 2 * x, 16 * j)])
    for xb, own, first in ((0, side_left, 0), (3, side_right, 8)):
        for yb in range(4):
            ref, at, row = ((corner_low, first, 0), (own, 0, 0), (own, 0, 8), (corner_high, first, 0))[yb]
            here = pl.ds(8 * yb + 8, 8)
            for b in range(4):
                tile = 6.0 * coupling[xb, b, here, :]
                for x in range(8):
                    drive[first + x, b, here, :] = tile * ref[at + x, row : row + 8, 128 * b : 128 * b + 128]

    def forcing(x):
        return (inner_drive, x) if 0 <= x < 16 else (drive, x + 8 if x < 0 else x - 8)

    def state(k, x):
        if k <= x < 16 - k:
            return (inner_odd if k % 2 else inner_even), x
        return (odd if k % 2 else even), x + 10

    for k in range(1, 9):
        for rows in (range(k - 9, k), range(16 - k, 25 - k)) if k < 8 else (range(-1, 17),):
            sweep(
                rows, fine_starts(k), 4,
                lambda x: state(k - 1, x),
                lambda x: state(k, x),
                forcing,
                lambda x: (coupling, x // 8 + 1),
            )
    copies = []
    for first in (0, 8):
        for start in (16, 24):
            def load(x, shift):
                return [even[x + 10, b, pl.ds(start + shift, 8), :] for b in range(4)]

            v, out = stencil_rows(load, range(first, first + 8), 4)
            for x in range(first, first + 8):
                for b in range(4):
                    lanes, rows = slice(128 * b, 128 * b + 128), slice(start - 16, start - 8)
                    center = center_ref[1 + x // 8, start // 8 - 1 : start // 8, lanes]
                    solution_ref[x, rows, lanes] = v[x][b]
                    residual_ref[x, rows, lanes] = (
                        side_ref[x, rows, lanes] - center * v[x][b] + (1.0 / 6.0) * out[x][b]
                    )
        part = pl.ds(first, 8)
        for n, (source, target) in enumerate(((solution_ref, solution_hbm), (residual_ref, residual_hbm))):
            copies.append(pltpu.make_async_copy(source.at[part], target.at[part], sent.at[first // 4 + n]))
            copies[-1].start()
    for copy in copies:
        copy.wait()


def shape(*dims):
    return jax.ShapeDtypeStruct(dims, F32)


def call(kernel, outputs, scratch, name, microseconds, **specs):
    cost = pl.CostEstimate(flops=int(microseconds * 1.0e9), bytes_accessed=int(microseconds * 3.69e6), transcendentals=0)
    return pl.pallas_call(
        kernel,
        out_shape=[shape(*dims) for dims in outputs],
        scratch_shapes=[pltpu.VMEM(dims, F32) if isinstance(dims, tuple) else dims for dims in scratch],
        compiler_params=pltpu.CompilerParams(vmem_limit_bytes=20 * 1024 * 1024),
        cost_estimate=cost,
        name=name,
        **specs,
    )


def shards(right_side, point_counts):
    def exchange(axis, to_low, to_high):
        count, even = lax.axis_size(axis), lax.axis_index(axis) % 2 == 0
        outer = [(i, (i + (-1 if i % 2 == 0 else 1)) % count) for i in range(count)]
        inner = [(i, i + (1 if i % 2 == 0 else -1)) for i in range(count)]
        same = to_low is to_high
        first = lax.ppermute(to_low if same else jnp.where(even, to_low, to_high), axis, outer)
        second = lax.ppermute(to_low if same else jnp.where(even, to_high, to_low), axis, inner)
        return jnp.where(even, first, second), jnp.where(even, second, first)

    (packed,) = call(
        restrict_kernel,
        [(9, 8, 256)],
        [(4, 128, 128), (16, 16, 512), pltpu.VMEM((2, 2, 64), jnp.int32), pltpu.SemaphoreType.DMA((2,))],
        "restrict",
        1,
        in_specs=[pl.BlockSpec(memory_space=pltpu.MemorySpace.HBM)] * 2,
    )(
        pltpu.with_memory_space_constraint(right_side, pltpu.MemorySpace.HBM),
        pltpu.with_memory_space_constraint(point_counts, pltpu.MemorySpace.HBM),
    )
    first, last = call(slices_kernel, [(8, 16, 512), (8, 16, 512)], [], "slices", 1)(packed, right_side)
    left, right = exchange("gx", packed, packed)
    packed = jnp.concatenate([left, packed, right], axis=0)
    side_left, side_right = exchange("gx", first, last)
    packed, own = lax.optimization_barrier((packed, right_side))
    side_low, side_high = exchange("gy", own[:, 0:8], own[:, 8:16])
    coarse, counts = call(
        coarse_kernel,
        [(8, 8, 256), (72, 128)],
        [(26, 2, 40, 128)] * 3 + [(6, 2, 40, 128)],
        "coarse",
        COARSE_US,
    )(packed, *exchange("gy", packed, packed))
    coarse, side_left, side_right = lax.optimization_barrier((coarse, side_left, side_right))
    coarse_low, coarse_high = exchange("gy", coarse, coarse)
    corner_low, corner_high = exchange(
        "gy",
        jnp.concatenate([side_left[:, 0:8], side_right[:, 0:8]], axis=0),
        jnp.concatenate([side_left[:, 8:16], side_right[:, 8:16]], axis=0),
    )
    wide = jnp.concatenate([coarse_low, coarse, coarse_high], axis=1)
    coarse_left, coarse_right = exchange("gx", wide[0:5], wide[3:8])
    field = (16, 4, 48, 128)
    even, odd, drive, coupling, center = call(
        inner_kernel, [field, field, field, (4, 4, 48, 128), (4, 4, 512)], [], "inner", INNER_US
    )(
        right_side, side_low, side_high, coarse, coarse_low, coarse_high, counts
    )
    field, block = (36, 4, 48, 128), (16, 16, 512)
    return call(
        outer_kernel,
        [block, block],
        [field, field, (16, 4, 48, 128), block, block, pltpu.SemaphoreType.DMA((4,))],
        "outer",
        6,
        out_specs=[pl.BlockSpec(memory_space=pltpu.MemorySpace.HBM)] * 2,
    )(
        right_side, side_left, side_right, corner_low, corner_high, coarse_left, coarse_right, center,
        even, odd, drive, coupling,
    )


def solution(mesh):
    specs = (P("gx", "gy", None), P("gx", "gy", None))
    return jax.shard_map(shards, mesh=mesh, in_specs=specs, out_specs=specs, check_vma=False)
```
